128 devices in a mesh: scan: 8 (over y, core), morton: 16 (over x, z).
Axes of the slice: x: 4, y: 4, z: 4, core: 2. Of those that a mesh axis runs over, the one named last changes fastest.
Arguments:
- positions: float32 [2048, 3, 128], P(('scan', 'morton')), may hold values from 0 to 7
- normals: float32 [2048, 3, 128], P(('scan', 'morton')), may hold values from -4 to 4
- weights: float32 [2048, 128], P(('scan', 'morton')), may hold values from 0.1 to 1
- point_target: int32 [2048], P(('scan', 'morton')), may hold values from 0 to 1023, as said below
- neighbours: int32 [1024, 27], P(('scan', 'morton')), may hold values from -1 to 1023, as said below
Outputs:
- solution_field: float32 [1024, 512], P(('scan', 'morton'))
- residual: float32 [1024, 512], P(('scan', 'morton'))
The draws below stay inside these ranges and needn't reach their ends.
Inputs may be any that keep to these rules, and one draw needn't show every extreme that they name: point_target[q] // 8 % 16 equals (q // 16) % 16; of the 16 point blocks of one device, at most 4 have the same point_target // (16 * 8), and exactly 4 for some value on every device. `neighbours`: entry 9 (a + 1) + 3 (b + 1) + (c + 1) of a block's row names the block across offset (a, b, c); the centre entry is the block itself; if block g names h at an offset, h names g at the opposite offset; a named block h of row g satisfies |h // 8 - g // 8| <= 1.
All inputs are finite; a program needn't handle non-finite values.
Results may differ from the reference program's by a relative error of at most 0.0003.
Values sent between devices are 32-bit elements; how exact they have to be, the bound alone decides.
No kernel may reach another device: no remote copies, remote signals or barrier semaphores. Data moves between devices by JAX's collectives and lax.ppermute only.
A program may use at most 128 MiB of HBM per device.

```python
import math
import jax
import jax.numpy as jnp
from jax import lax

PTS = 128
ITERS = 2
PB_DEV = 16
BLK_DEV = 8
NPB = 2048
NBLOCKS = 1024
N_SCAN = 8
N_MORTON = 16
DEVICES = 128


def draw_point_target(key, part):
    row_cap = max(2, 2 * PB_DEV // N_SCAN)
    width = N_SCAN * row_cap
    key_forced, key_score, key_mix, key_slot = jax.random.split(jax.random.fold_in(key, 3), 4)
    forced = jax.random.randint(key_forced, (DEVICES,), 0, N_SCAN).astype(jnp.int32)
    forced = forced.at[0].set(0).at[DEVICES - 1].set(N_SCAN - 1)
    places = jnp.arange(width, dtype=jnp.int32)
    random_score = jax.random.randint(key_score, (DEVICES, width), 0, 2 ** 18).astype(jnp.int32)
    score = jnp.where((places // row_cap)[None, :] == forced[:, None], places[None, :] - 4096, random_score * 4096 + places[None, :])
    chosen = jnp.argsort(score, axis=1)[:, :PB_DEV].astype(jnp.int32)
    row_pick = chosen // row_cap
    mix_score = jax.random.randint(key_mix, (DEVICES, PB_DEV), 0, 2 ** 18).astype(jnp.int32) * 4096 + jnp.arange(PB_DEV, dtype=jnp.int32)[None, :]
    mixing = jnp.argsort(mix_score, axis=1).astype(jnp.int32)
    row = jnp.take_along_axis(row_pick, mixing, axis=1).reshape(NPB).astype(jnp.int32)
    serial = jnp.arange(NPB, dtype=jnp.int32)
    device = serial // PB_DEV
    column = device % N_MORTON
    slot = jax.random.randint(key_slot, (NPB,), 0, BLK_DEV).astype(jnp.int32)
    slot = jnp.where((device == 0) & (row == 0), 0, jnp.where((device == DEVICES - 1) & (row == N_SCAN - 1), BLK_DEV - 1, slot))
    return (row * N_MORTON * BLK_DEV + column * BLK_DEV + slot).astype(jnp.int32)


def draw_neighbours(key, part):
    side = 1
    while (side + 1) * (side + 1) + (side + 1) + 1 <= BLK_DEV:
        side = side + 1
    owners = NBLOCKS // BLK_DEV
    key_perm, key_drop = jax.random.split(jax.random.fold_in(key, 7))
    perms = jax.vmap(lambda k: jax.random.permutation(k, BLK_DEV))(jax.random.split(key_perm, owners)).astype(jnp.int32)
    spot = jnp.arange(NBLOCKS, dtype=jnp.int32)

    def ident(place):
        return place // BLK_DEV * BLK_DEV + perms[place // BLK_DEV, place % BLK_DEV]
    xs = spot % side
    ys = spot // side % side
    loose = jax.random.randint(key_drop, (NBLOCKS, 27), 0, 100) < 15
    columns = []
    for k in range(27):
        a = k // 9 - 1
        b = k // 3 % 3 - 1
        c = k % 3 - 1
        other = spot + a + b * side + c * side * side
        valid = (xs + a >= 0) & (xs + a < side) & (ys + b >= 0) & (ys + b < side) & (other >= 0) & (other < NBLOCKS)
        safe = jnp.clip(other, 0, NBLOCKS - 1)
        lower = jnp.minimum(spot, safe)
        canon = jnp.where(safe > spot, k, 26 - k)
        cut = loose[lower, canon] & (k != 13)
        columns.append(jnp.where(valid & jnp.logical_not(cut), ident(safe), -1))
    table = jnp.stack(columns, axis=1).astype(jnp.int32)
    return jnp.zeros((NBLOCKS, 27), jnp.int32).at[ident(spot)].set(table)


def levels(key, shape, cuts, least, high):
    def one(dim, shards_of):
        heights = jax.random.uniform(jax.random.fold_in(jax.random.fold_in(key, 6), dim), (shards_of,), jnp.float32, least / len(cuts), high / len(cuts))
        return jnp.repeat(jnp.exp(heights), shape[dim] // shards_of).reshape((-1,) + (1,) * (len(shape) - dim - 1))

    loudness = one(*cuts[0])
    for cut in cuts[1:]:
        loudness = loudness * one(*cut)
    return loudness


def noise(own_key, shape, scale, limit, cuts=(), kind=jnp.bfloat16):
    values = scale * jax.random.normal(own_key, shape, jnp.float32)
    if cuts:
        values = values * levels(own_key, shape, cuts, -0.22, 0.18)
    return jnp.clip(values, -limit, limit).astype(kind)


def setup_inputs(seed: int = 0) -> dict:
    key_list = jax.random.split(jax.random.key(seed), 6)
    return {
        "positions": jnp.clip(7.0 * jax.random.uniform(key_list[0], (NPB, 3, PTS), jnp.float32) ** levels(key_list[0], (NPB, 3, PTS), ((0, 128),), -0.2, 0.2), 0.0, 7.0),
        "normals": noise(key_list[1], (NPB, 3, PTS), 1.0, 4.0, ((0, 128),), jnp.float32),
        "weights": jnp.clip(jnp.exp(math.log(1.0) - 2.3025851 * jax.random.uniform(key_list[2], (NPB, PTS), jnp.float32) ** levels(key_list[2], (NPB, PTS), ((0, 128),), -0.2, 0.2)), 0.1, 1.0),
        "point_target": draw_point_target(jax.random.fold_in(key_list[5], 71), 0),
        "neighbours": draw_neighbours(jax.random.fold_in(key_list[5], 71), 0),
    }


SCREEN = 16.0


def splat(positions, normals, weights):
    count = positions.shape[0]
    group = math.gcd(count, 16)

    def one(pack):
        spots, norms, wts = pack
        nodes = jnp.arange(8).astype(spots.dtype)
        diff = spots[:, :, :, None] - nodes
        dist = jnp.abs(diff)
        hat = jnp.maximum(0.0, 1.0 - dist)
        slope = jnp.where(dist < 1.0, -jnp.sign(diff), 0.0)
        wn = wts[:, :, None]
        left = jnp.stack([wn * norms[:, 0, :, None] * slope[:, 0], wn * hat[:, 0]], axis=2)
        first = hat[:, 1, :, :, None] * hat[:, 2, :, None, :]
        second = norms[:, 1, :, None, None] * slope[:, 1, :, :, None] * hat[:, 2, :, None, :] + norms[:, 2, :, None, None] * hat[:, 1, :, :, None] * slope[:, 2, :, None, :]
        right = jnp.stack([first, second], axis=2)
        rhs = jnp.einsum('gpti,gptjk->gijk', left, right, precision=lax.Precision.HIGHEST)
        squares = hat * hat
        outer = squares[:, 1, :, :, None] * squares[:, 2, :, None, :]
        scr = SCREEN * jnp.einsum('gpi,gpjk->gijk', wn * squares[:, 0], outer, precision=lax.Precision.HIGHEST)
        return rhs.reshape(group, 512), scr.reshape(group, 512)

    packs = (positions.reshape(count // group, group, 3, -1), normals.reshape(count // group, group, 3, -1), weights.reshape(count // group, group, -1))
    rhs, scr = lax.map(one, packs)
    return rhs.reshape(count, 512), scr.reshape(count, 512)


def coefficient(a, b, c):
    mass = {-1: 1.0 / 6.0, 0: 2.0 / 3.0, 1: 1.0 / 6.0}
    stiff = {-1: -1.0, 0: 2.0, 1: -1.0}
    return stiff[a] * mass[b] * mass[c] + mass[a] * stiff[b] * mass[c] + mass[a] * mass[b] * stiff[c]


def assemble(nearby):
    blocks = nearby.shape[0]
    cube = nearby.reshape(blocks, 27, 8, 8, 8)
    cuts = {-1: (7, 8), 0: (0, 8), 1: (0, 1)}
    planes = []
    for a in (-1, 0, 1):
        rows = []
        for b in (-1, 0, 1):
            cols = []
            for c in (-1, 0, 1):
                piece = cube[:, (a + 1) * 9 + (b + 1) * 3 + (c + 1)]
                piece = piece[:, cuts[a][0]:cuts[a][1], cuts[b][0]:cuts[b][1], cuts[c][0]:cuts[c][1]]
                cols.append(piece)
            rows.append(jnp.concatenate(cols, axis=3))
        planes.append(jnp.concatenate(rows, axis=2))
    return jnp.concatenate(planes, axis=1)


def stencil(padded, screen, field):
    blocks = field.shape[0]
    out = screen.reshape(blocks, 8, 8, 8) * field.reshape(blocks, 8, 8, 8)
    for a in (-1, 0, 1):
        for b in (-1, 0, 1):
            for c in (-1, 0, 1):
                weight = coefficient(a, b, c)
                if weight != 0.0:
                    out = out + weight * padded[:, 1 + a:9 + a, 1 + b:9 + b, 1 + c:9 + c]
    return out.reshape(blocks, 512)


def reference(positions, normals, weights, point_target, neighbours):
    rhs_part, screen_part = splat(positions, normals, weights)
    rhs = jax.ops.segment_sum(rhs_part, point_target, num_segments=NBLOCKS)
    screen = jax.ops.segment_sum(screen_part, point_target, num_segments=NBLOCKS)
    index = jnp.where(neighbours >= 0, neighbours, NBLOCKS).astype(jnp.int32)

    def operate(field):
        table = jnp.concatenate([field, jnp.zeros((1, 512), field.dtype)], axis=0)
        return stencil(assemble(table[index]), screen, field)

    solution_field = jnp.zeros_like(rhs)
    residual, direction = rhs, rhs
    norm_now = jnp.sum(residual * residual)
    for step in range(ITERS):
        image = operate(direction)
        alpha = norm_now / jnp.sum(direction * image)
        solution_field = solution_field + alpha * direction
        residual = residual - alpha * image
        norm_next = jnp.sum(residual * residual)
        direction = residual + (norm_next / norm_now) * direction
        norm_now = norm_next
    return solution_field, residual
```

```python
import jax
import jax.numpy as jnp
import numpy as np
from jax import lax
from jax.experimental import pallas as pl
from jax.experimental.pallas import tpu as pltpu
from jax.sharding import PartitionSpec as P

SCREEN = 16.0
BLOCKS = 8
SLOTS = 4
SHARE = SLOTS * 8 + 8
BOTH = ("scan", "morton")


def plane_table():
    mass = {-1: 1.0, 0: 4.0, 1: 1.0}
    stiff = {-1: -1.0, 0: 2.0, 1: -1.0}
    table = np.zeros((640, 128), np.float32)
    for b in (-1, 0, 1):
        for c in (-1, 0, 1):
            for row in range(64):
                for col in range(64):
                    dj = 8 * b + row // 8 - col // 8
                    dk = 8 * c + row % 8 - col % 8
                    if abs(dj) > 1 or abs(dk) > 1:
                        continue
                    at = 64 * (3 * (b + 1) + (c + 1)) + row
                    table[at, col] = mass[dj] * mass[dk]
                    table[at, 64 + col] = stiff[dj] * mass[dk] + mass[dj] * stiff[dk]
    return table


def split(values):
    high = values.astype(jnp.bfloat16)
    low = (values - high.astype(jnp.float32)).astype(jnp.bfloat16)
    return high, low


def nt(left, right):
    return lax.dot_general(left, right, (((1,), (1,)), ((), ())), preferred_element_type=jnp.float32)


def left_half():
    return lax.broadcasted_iota(jnp.int32, (8, 128), 1) < 64


def splat_kernel(target_ref, spots_ref, norms_ref, weights_ref, out_ref, used_ref):
    node = lax.broadcasted_iota(jnp.int32, (8, 128), 0).astype(jnp.float32)
    first_half = left_half()
    nothing = jnp.zeros((64, 128), jnp.float32)
    for row in range(8):
        used_ref[row] = 0
        out_ref[row * SHARE + SLOTS * 8 : (row + 1) * SHARE, :] = jnp.full((8, 128), -1.0, jnp.float32)
    for q in range(16):
        hats, slopes = [], []
        for dim in range(3):
            diff = spots_ref[q, dim : dim + 1, :] - node
            dist = jnp.abs(diff)
            hats.append(jnp.maximum(0.0, 1.0 - dist))
            way = jnp.where(diff > 0.0, -1.0, jnp.where(diff < 0.0, 1.0, 0.0))
            slopes.append(jnp.where(dist < 1.0, way, 0.0))
        weight = weights_ref[q : q + 1, :]
        one = weight * norms_ref[q, 0:1, :] * slopes[0]
        two = weight * hats[0]
        three = SCREEN * two * hats[0]
        slope1 = norms_ref[q, 1:2, :] * slopes[1]
        slope2 = norms_ref[q, 2:3, :] * slopes[2]
        square1 = hats[1] * hats[1]
        square2 = hats[2] * hats[2]
        first = jnp.concatenate([hats[1][j : j + 1] * hats[2] for j in range(8)], axis=0)
        second = jnp.concatenate(
            [slope1[j : j + 1] * hats[2] + hats[1][j : j + 1] * slope2 for j in range(8)], axis=0
        )
        outer = jnp.concatenate([square1[j : j + 1] * square2 for j in range(8)], axis=0)
        right = jnp.concatenate(
            [jnp.concatenate([first, second], axis=1), jnp.concatenate([outer, nothing], axis=1)], axis=0
        )
        left = jnp.concatenate(
            [
                jnp.concatenate([one, two], axis=1),
                jnp.concatenate([three, jnp.zeros((8, 128), jnp.float32)], axis=1),
            ],
            axis=0,
        )
        right_high, right_low = split(right)
        left_high, left_low = split(left)
        main = nt(jnp.concatenate([left_high, left_low], axis=0), right_high)
        total = main[:16] + main[16:] + nt(left_high, right_low)
        target = target_ref[q]
        row = target // (16 * BLOCKS)
        slot = used_ref[row]
        used_ref[row] = slot + 1
        place = pl.multiple_of(row * SHARE + slot * 8, 8)
        out_ref[pl.ds(place, 8), :] = jnp.where(first_half, total[:8], total[8:])
        block = (target % BLOCKS).astype(jnp.float32)
        out_ref[pl.ds(row * SHARE + SLOTS * 8 + slot, 1), :] = jnp.full((1, 128), block, jnp.float32)


def combine_kernel(parts_ref, out_ref):
    sums = [jnp.zeros((8, 128), jnp.float32) for _ in range(BLOCKS)]
    for source in range(8):
        for slot in range(SLOTS):
            at = source * SHARE
            part = parts_ref[at + slot * 8 : at + slot * 8 + 8, :]
            name = jnp.broadcast_to(parts_ref[at + SLOTS * 8 + slot : at + SLOTS * 8 + slot + 1, :], (8, 128))
            for block in range(BLOCKS):
                sums[block] = sums[block] + jnp.where(name == float(block), part, 0.0)
    for block in range(BLOCKS):
        out_ref[block] = sums[block]


def doubled(tile, first_half):
    return jnp.where(first_half, tile, pltpu.roll(tile, 64, 1))


def couple(near_ref, wide_ref, planes_ref, rows_ref, table_ref):
    first_half = left_half()
    first_row = first_half[:1]
    me = lax.axis_index("scan") * lax.axis_size("morton") + lax.axis_index("morton")
    base = (me - 1) * BLOCKS

    def place(block, offset):
        named = near_ref[block, offset]
        return jnp.where(named < 0, 3 * BLOCKS, named - base)

    for block in range(BLOCKS):
        for pair in range(5):
            lanes = slice(128 * pair, 128 * pair + 128)
            for shift, plane, at in ((0, 7, 64 + block), (9, None, 8 * block), (18, 0, 72 + block)):
                rows = slice(0, 8) if plane is None else slice(plane, plane + 1)
                tile = wide_ref[place(block, shift + 2 * pair), rows, :]
                if pair < 4:
                    other = wide_ref[place(block, shift + 2 * pair + 1), rows, :]
                    tile = jnp.where(first_half if plane is None else first_row, tile, other)
                rows_ref[at : at + tile.shape[0], lanes] = tile
    high, low = split(rows_ref[...])
    both = jnp.dot(
        jnp.concatenate([high, low], axis=0), table_ref[...], preferred_element_type=jnp.float32
    )
    sums = both[:80] + both[80:]
    result = []
    centre = jnp.where(first_half, 2.0 / 36.0, 4.0 / 36.0)
    side = jnp.where(first_half, -1.0 / 36.0, 1.0 / 36.0)
    for block in range(BLOCKS):
        planes_ref[block, 1:9, :] = sums[8 * block : 8 * block + 8]
        planes_ref[block, 0:1, :] = sums[64 + block : 65 + block]
        planes_ref[block, 9:10, :] = sums[72 + block : 73 + block]
    for block in range(BLOCKS):
        around = planes_ref[block, 0:8, :] + planes_ref[block, 2:10, :]
        value = centre * sums[8 * block : 8 * block + 8] + side * around
        result.append(value + pltpu.roll(value, 64, 1))
    return result


def fill(wide_ref, own_ref, before_ref, after_ref, first_half):
    for block in range(BLOCKS):
        wide_ref[block] = doubled(before_ref[block], first_half)
        wide_ref[BLOCKS + block] = doubled(own_ref[block], first_half)
        wide_ref[2 * BLOCKS + block] = doubled(after_ref[block], first_half)
    wide_ref[3 * BLOCKS] = jnp.zeros((8, 128), jnp.float32)


def image_of(own_ref, before_ref, after_ref, fields_ref, near_ref, table_ref, wide_ref, rows_ref, planes_ref):
    first_half = left_half()
    fill(wide_ref, own_ref, before_ref, after_ref, first_half)
    coupled = couple(near_ref, wide_ref, planes_ref, rows_ref, table_ref)
    images = []
    for block in range(BLOCKS):
        tile = fields_ref[block]
        screen = jnp.where(first_half, pltpu.roll(tile, 64, 1), tile)
        images.append(screen * wide_ref[BLOCKS + block] + coupled[block])
    return images


def first_kernel(near_ref, fields_ref, before_ref, after_ref, table_ref, out_ref, wide_ref, rows_ref, planes_ref):
    images = image_of(
        fields_ref, before_ref, after_ref, fields_ref, near_ref, table_ref, wide_ref, rows_ref, planes_ref
    )
    for block in range(BLOCKS):
        out_ref[block] = images[block]


def total(lefts, rights, first_half):
    terms = [a * b for a, b in zip(lefts, rights)]
    while len(terms) > 1:
        terms = [a + b for a, b in zip(terms[::2], terms[1::2])]
    return jnp.sum(jnp.where(first_half, terms[0], 0.0), axis=(0, 1), keepdims=True)


def second_kernel(
    near_ref, own_ref, before_ref, after_ref, fields_ref, table_ref, out_ref, sums_ref, wide_ref, rows_ref, planes_ref
):
    second = image_of(
        own_ref, before_ref, after_ref, fields_ref, near_ref, table_ref, wide_ref, rows_ref, planes_ref
    )
    first_half = left_half()
    start = [fields_ref[block] for block in range(BLOCKS)]
    first = [own_ref[block] for block in range(BLOCKS)]
    lane = lax.broadcasted_iota(jnp.int32, (1, 128), 1)
    packed = jnp.zeros((1, 128), jnp.float32)
    pairs = ((start, start), (start, first), (first, first), (start, second), (first, second))
    for place, (a, b) in enumerate(pairs):
        packed = jnp.where(lane == place, total(a, b, first_half), packed)
    sums_ref[...] = jnp.broadcast_to(packed, (128, 128))
    for block in range(BLOCKS):
        out_ref[block] = second[block]


def last_kernel(sums_ref, fields_ref, first_ref, second_ref, solution_ref, residual_ref, left_ref, right_ref):
    first_half = left_half()
    sums = jnp.sum(sums_ref[...], axis=0, keepdims=True)
    lane = lax.broadcasted_iota(jnp.int32, (1, 128), 1)

    def pick(place):
        return jnp.sum(jnp.where(lane == place, sums, 0.0), axis=1, keepdims=True)

    s00, s01, s11, s02, s12 = (pick(place) for place in range(5))
    alpha0 = s00 / s01
    norm1 = s00 - 2.0 * alpha0 * s01 + alpha0 * alpha0 * s11
    beta = norm1 / s00
    grow = 1.0 + beta
    curve = grow * grow * s01 - grow * alpha0 * (s02 + s11) + alpha0 * alpha0 * s12
    alpha1 = norm1 / curve
    for block in range(BLOCKS):
        start = doubled(fields_ref[block], first_half)
        first = first_ref[block]
        left = start - alpha0 * first
        direction = left + beta * start
        image = grow * first - alpha0 * second_ref[block]
        left_ref[block] = alpha0 * start + alpha1 * direction
        right_ref[block] = left - alpha1 * image
    for pair in range(4):
        lanes = slice(128 * pair, 128 * pair + 128)
        solution_ref[:, lanes] = jnp.where(first_half, left_ref[:, 2 * pair, :], left_ref[:, 2 * pair + 1, :])
        residual_ref[:, lanes] = jnp.where(first_half, right_ref[:, 2 * pair, :], right_ref[:, 2 * pair + 1, :])


def vmem(count):
    return [pl.BlockSpec(memory_space=pltpu.VMEM)] * count


def smem(count):
    return [pl.BlockSpec(memory_space=pltpu.SMEM)] * count


def shape(*dims):
    return jax.ShapeDtypeStruct(dims, jnp.float32)


STENCIL_SCRATCH = [
    pltpu.VMEM((3 * BLOCKS + 1, 8, 128), jnp.float32),
    pltpu.VMEM((80, 640), jnp.float32),
    pltpu.VMEM((BLOCKS, 16, 128), jnp.float32),
]


def around(values):
    count = lax.axis_size("scan") * lax.axis_size("morton")
    up = [(i, i + 1) for i in range(count - 1)]
    down = [(i + 1, i) for i in range(count - 1)]
    return lax.ppermute(values, BOTH, up), lax.ppermute(values, BOTH, down)


def per_device(positions, normals, weights, point_target, neighbours):
    table = jnp.asarray(plane_table(), jnp.bfloat16)
    parts = pl.pallas_call(
        splat_kernel,
        out_shape=shape(8 * SHARE, 128),
        in_specs=smem(1) + vmem(3),
        out_specs=vmem(1)[0],
        scratch_shapes=[pltpu.SMEM((8,), jnp.int32)],
        name="splat",
    )(point_target, positions, normals, weights)
    parts = lax.all_to_all(parts, "scan", 0, 0, tiled=True)
    fields = pl.pallas_call(
        combine_kernel, out_shape=shape(BLOCKS, 8, 128), in_specs=vmem(1), out_specs=vmem(1)[0], name="combine"
    )(parts)
    before, after = around(fields)
    first = pl.pallas_call(
        first_kernel,
        out_shape=shape(BLOCKS, 8, 128),
        in_specs=smem(1) + vmem(4),
        out_specs=vmem(1)[0],
        scratch_shapes=STENCIL_SCRATCH,
        name="first",
    )(neighbours, fields, before, after, table)
    before, after = around(first)
    second, sums = pl.pallas_call(
        second_kernel,
        out_shape=(shape(BLOCKS, 8, 128), shape(128, 128)),
        in_specs=smem(1) + vmem(5),
        out_specs=tuple(vmem(2)),
        scratch_shapes=STENCIL_SCRATCH,
        name="second",
    )(neighbours, first, before, after, fields, table)
    sums = lax.all_to_all(sums, BOTH, 0, 0, tiled=True)
    return pl.pallas_call(
        last_kernel,
        out_shape=(shape(BLOCKS, 512), shape(BLOCKS, 512)),
        in_specs=vmem(4),
        out_specs=tuple(vmem(2)),
        scratch_shapes=[pltpu.VMEM((BLOCKS, 8, 128), jnp.float32)] * 2,
        name="last",
    )(sums, fields, first, second)


def solution(mesh):
    placed = (
        P(BOTH, None, None),
        P(BOTH, None, None),
        P(BOTH, None),
        P(BOTH),
        P(BOTH, None),
    )
    return jax.shard_map(
        per_device,
        mesh=mesh,
        in_specs=placed,
        out_specs=(P(BOTH, None), P(BOTH, None)),
        check_vma=False,
    )
```

```python
import jax
import jax.numpy as jnp
import numpy as np
from jax import lax
from jax.experimental import pallas as pl
from jax.experimental.pallas import tpu as pltpu
from jax.sharding import PartitionSpec as P

SCREEN = 16.0
BLOCKS = 8
SLOTS = 4
SHARE = SLOTS * 8 + 8
BOTH = ("scan", "morton")


def plane_table():
    mass = {-1: 1.0, 0: 4.0, 1: 1.0}
    stiff = {-1: -1.0, 0: 2.0, 1: -1.0}
    side = {0: 1, 7: -1}
    table = np.zeros((256, 128), np.float32)
    for group in range(4):
        for row in range(64):
            b = side.get(row // 8) if group in (1, 3) else 0
            c = side.get(row % 8) if group in (2, 3) else 0
            if b is None or c is None:
                continue
            for col in range(64):
                dj = 8 * b + row // 8 - col // 8
                dk = 8 * c + row % 8 - col % 8
                if abs(dj) <= 1 and abs(dk) <= 1:
                    table[64 * group + row, col] = mass[dj] * mass[dk]
                    table[64 * group + row, 64 + col] = stiff[dj] * mass[dk] + mass[dj] * stiff[dk]
    return table


def split(values):
    high = values.astype(jnp.bfloat16)
    low = (values - high.astype(jnp.float32)).astype(jnp.bfloat16)
    return high, low


def nt(left, right):
    return lax.dot_general(left, right, (((1,), (1,)), ((), ())), preferred_element_type=jnp.float32)


def left_half():
    return lax.broadcasted_iota(jnp.int32, (8, 128), 1) < 64


def splat_kernel(target_ref, spots_ref, norms_ref, weights_ref, out_ref, used_ref):
    node = lax.broadcasted_iota(jnp.int32, (8, 128), 0).astype(jnp.float32)
    first_half = left_half()
    nothing = jnp.zeros((64, 128), jnp.float32)
    for row in range(8):
        used_ref[row] = 0
        out_ref[row * SHARE + SLOTS * 8 : (row + 1) * SHARE, :] = jnp.full((8, 128), -1.0, jnp.float32)
    for q in range(16):
        hats, slopes = [], []
        for dim in range(3):
            diff = spots_ref[dim, q : q + 1, :] - node
            dist = jnp.abs(diff)
            hats.append(jnp.maximum(0.0, 1.0 - dist))
            way = jnp.where(diff > 0.0, -1.0, jnp.where(diff < 0.0, 1.0, 0.0))
            slopes.append(jnp.where(dist < 1.0, way, 0.0))
        weight = weights_ref[q : q + 1, :]
        one = weight * norms_ref[0, q : q + 1, :] * slopes[0]
        two = weight * hats[0]
        three = SCREEN * two * hats[0]
        slope1 = norms_ref[1, q : q + 1, :] * slopes[1]
        slope2 = norms_ref[2, q : q + 1, :] * slopes[2]
        square1 = hats[1] * hats[1]
        square2 = hats[2] * hats[2]
        first = jnp.concatenate([hats[1][j : j + 1] * hats[2] for j in range(8)], axis=0)
        second = jnp.concatenate(
            [slope1[j : j + 1] * hats[2] + hats[1][j : j + 1] * slope2 for j in range(8)], axis=0
        )
        outer = jnp.concatenate([square1[j : j + 1] * square2 for j in range(8)], axis=0)
        right = jnp.concatenate(
            [jnp.concatenate([first, second], axis=1), jnp.concatenate([outer, nothing], axis=1)], axis=0
        )
        left = jnp.concatenate(
            [
                jnp.concatenate([one, two], axis=1),
                jnp.concatenate([three, jnp.zeros((8, 128), jnp.float32)], axis=1),
            ],
            axis=0,
        )
        right_high, right_low = split(right)
        left_high, left_low = split(left)
        main = nt(jnp.concatenate([left_high, left_low], axis=0), right_high)
        total = main[:16] + main[16:] + nt(left_high, right_low)
        target = target_ref[q]
        row = target // (16 * BLOCKS)
        slot = used_ref[row]
        used_ref[row] = slot + 1
        place = pl.multiple_of(row * SHARE + slot * 8, 8)
        out_ref[pl.ds(place, 8), :] = jnp.where(first_half, total[:8], total[8:])
        block = (target % BLOCKS).astype(jnp.float32)
        out_ref[pl.ds(row * SHARE + SLOTS * 8 + slot, 1), :] = jnp.full((1, 128), block, jnp.float32)


def combine_kernel(parts_ref, near_ref, out_ref):
    sums = [jnp.zeros((8, 128), jnp.float32) for _ in range(BLOCKS)]
    for source in range(8):
        for slot in range(SLOTS):
            at = source * SHARE
            part = parts_ref[at + slot * 8 : at + slot * 8 + 8, :]
            name = jnp.broadcast_to(parts_ref[at + SLOTS * 8 + slot : at + SLOTS * 8 + slot + 1, :], (8, 128))
            for block in range(BLOCKS):
                sums[block] = sums[block] + jnp.where(name == float(block), part, 0.0)
    for block in range(BLOCKS):
        out_ref[block] = sums[block]
    out_ref[BLOCKS] = jnp.full((8, 128), -1.0, jnp.float32)
    out_ref[BLOCKS, :, 0:27] = near_ref[...].astype(jnp.float32)


def doubled(tile, first_half):
    return jnp.where(first_half, tile, pltpu.roll(tile, 64, 1))


def couple(index_ref, first_row, blocks, wide_ref, rows_ref, table_ref):
    lane = lax.broadcasted_iota(jnp.int32, (8, 128), 1)
    sublane = lax.broadcasted_iota(jnp.int32, (8, 128), 0)
    first_half = lane < 64
    low_j = lane % 64 < 32
    low_k = lane % 8 < 4
    top = sublane == 0
    bottom = sublane == 7

    def tiles(block, shift):
        def plane(b, c):
            return wide_ref[index_ref[first_row + block, shift + 3 * (b + 1) + c + 1]]

        one = jnp.where(first_half, plane(0, 0), jnp.where(low_j, plane(1, 0), plane(-1, 0)))
        edges = jnp.where(low_k, plane(0, 1), plane(0, -1))
        corners = jnp.where(
            low_j,
            jnp.where(low_k, plane(1, 1), plane(1, -1)),
            jnp.where(low_k, plane(-1, 1), plane(-1, -1)),
        )
        return one, jnp.where(first_half, edges, corners)

    for block in range(blocks):
        before = tiles(block, 0)
        here = tiles(block, 9)
        after = tiles(block, 18)
        ends = [jnp.where(top, late, early) for early, late in zip(before, after)]
        rows = jnp.concatenate(
            [jnp.concatenate([here[half], ends[half]], axis=0) for half in range(2)], axis=1
        )
        high, low = split(rows)
        rows_ref[16 * block : 16 * block + 16, :] = high
        rows_ref[16 * (blocks + block) : 16 * (blocks + block) + 16, :] = low
    both = jnp.dot(rows_ref[0 : 32 * blocks, :], table_ref[...], preferred_element_type=jnp.float32)
    centre = jnp.where(first_half, 2.0 / 36.0, 4.0 / 36.0)
    side = jnp.where(first_half, -1.0 / 36.0, 1.0 / 36.0)
    result = []
    for block in range(blocks):
        at, other = 16 * block, 16 * (blocks + block)
        here = both[at : at + 8] + both[other : other + 8]
        ends = both[at + 8 : at + 16] + both[other + 8 : other + 16]
        before = pltpu.roll(jnp.where(bottom, ends, here), 1, 0)
        after = pltpu.roll(jnp.where(top, ends, here), 7, 0)
        value = centre * here + side * (before + after)
        result.append(value + pltpu.roll(value, 64, 1))
    return result


def total(lefts, rights, first_half):
    terms = [a * b for a, b in zip(lefts, rights)]
    while len(terms) > 1:
        terms = [a + b for a, b in zip(terms[::2], terms[1::2])]
    return jnp.sum(jnp.where(first_half, terms[0], 0.0), axis=(0, 1), keepdims=True)


def image_kernel(
    own_ref,
    one_ref,
    other_ref,
    far_ref,
    rest_ref,
    table_ref,
    first_ref,
    second_ref,
    sums_ref,
    wide_ref,
    next_ref,
    screen_ref,
    names_ref,
    index_ref,
    rows_ref,
    done_ref,
):
    first_half = left_half()
    me = lax.axis_index("scan") * lax.axis_size("morton") + lax.axis_index("morton")
    odd = lax.rem(me, 2)
    late = lax.rem(me, 4) // 2
    base = (me - 2) * BLOCKS
    near = ((own_ref, 2), (one_ref, 3 - 2 * odd), (other_ref, 1 + 2 * odd))
    far = ((far_ref, 4 - 4 * late), (rest_ref, 4 * late))
    for ref, place in near:
        named = ref[BLOCKS].astype(jnp.int32)
        local = named - base
        known = (named >= 0) & (local >= 0) & (local < 5 * BLOCKS)
        names_ref[pl.ds(pl.multiple_of((place - 1) * BLOCKS, 8), 8), :] = jnp.where(known, local, 5 * BLOCKS)
    copy = pltpu.make_async_copy(names_ref, index_ref, done_ref)
    copy.start()
    for ref, place in near + far:
        for block in range(BLOCKS):
            wide_ref[place * BLOCKS + block] = doubled(ref[block], first_half)
    for ref, place in near:
        for block in range(BLOCKS):
            tile = ref[block]
            screen_ref[(place - 1) * BLOCKS + block] = jnp.where(first_half, pltpu.roll(tile, 64, 1), tile)
    nothing = jnp.zeros((8, 128), jnp.float32)
    wide_ref[5 * BLOCKS] = nothing
    next_ref[5 * BLOCKS] = nothing
    copy.wait()
    coupled = couple(index_ref, 0, 3 * BLOCKS, wide_ref, rows_ref, table_ref)
    first = []
    for block in range(3 * BLOCKS):
        image = screen_ref[block] * wide_ref[BLOCKS + block] + coupled[block]
        next_ref[BLOCKS + block] = image
        if BLOCKS <= block < 2 * BLOCKS:
            first_ref[block - BLOCKS] = image
            first.append(image)
    coupled = couple(index_ref, BLOCKS, BLOCKS, next_ref, rows_ref, table_ref)
    second = []
    for block in range(BLOCKS):
        image = screen_ref[BLOCKS + block] * first[block] + coupled[block]
        second_ref[block] = image
        second.append(image)
    start = [wide_ref[2 * BLOCKS + block] for block in range(BLOCKS)]
    lane = lax.broadcasted_iota(jnp.int32, (1, 128), 1)
    packed = jnp.zeros((1, 128), jnp.float32)
    pairs = ((start, start), (start, first), (first, first), (start, second), (first, second))
    for place, (a, b) in enumerate(pairs):
        packed = jnp.where(lane == place, total(a, b, first_half), packed)
    sums_ref[...] = jnp.broadcast_to(packed, (128, 128))


def last_kernel(sums_ref, fields_ref, first_ref, second_ref, solution_ref, residual_ref, left_ref, right_ref):
    first_half = left_half()
    sums = jnp.sum(sums_ref[...], axis=0, keepdims=True)
    lane = lax.broadcasted_iota(jnp.int32, (1, 128), 1)

    def pick(place):
        return jnp.sum(jnp.where(lane == place, sums, 0.0), axis=1, keepdims=True)

    s00, s01, s11, s02, s12 = (pick(place) for place in range(5))
    alpha0 = s00 / s01
    norm1 = s00 - 2.0 * alpha0 * s01 + alpha0 * alpha0 * s11
    beta = norm1 / s00
    grow = 1.0 + beta
    curve = grow * grow * s01 - grow * alpha0 * (s02 + s11) + alpha0 * alpha0 * s12
    alpha1 = norm1 / curve
    for block in range(BLOCKS):
        start = doubled(fields_ref[block], first_half)
        first = first_ref[block]
        left = start - alpha0 * first
        direction = left + beta * start
        image = grow * first - alpha0 * second_ref[block]
        left_ref[block] = alpha0 * start + alpha1 * direction
        right_ref[block] = left - alpha1 * image
    for pair in range(4):
        lanes = slice(128 * pair, 128 * pair + 128)
        solution_ref[:, lanes] = jnp.where(first_half, left_ref[:, 2 * pair, :], left_ref[:, 2 * pair + 1, :])
        residual_ref[:, lanes] = jnp.where(first_half, right_ref[:, 2 * pair, :], right_ref[:, 2 * pair + 1, :])


def vmem(count):
    return [pl.BlockSpec(memory_space=pltpu.VMEM)] * count


def smem(count):
    return [pl.BlockSpec(memory_space=pltpu.SMEM)] * count


def shape(*dims):
    return pltpu.VMEM(dims, jnp.float32)


def resident(values):
    return pltpu.with_memory_space_constraint(values, pltpu.VMEM)


def around(values):
    count = lax.axis_size("scan") * lax.axis_size("morton")
    partners = (
        [i ^ 1 for i in range(count)],
        [(((i + 1) ^ 1) - 1) % count for i in range(count)],
        [i ^ 2 for i in range(count)],
        [(((i + 2) ^ 2) - 2) % count for i in range(count)],
    )
    return [resident(lax.ppermute(values, BOTH, list(enumerate(partner)))) for partner in partners]


def per_device(positions, normals, weights, point_target, neighbours):
    table = resident(jnp.asarray(plane_table(), jnp.bfloat16))
    parts = pl.pallas_call(
        splat_kernel,
        out_shape=shape(8 * SHARE, 128),
        in_specs=smem(1) + vmem(3),
        out_specs=vmem(1)[0],
        scratch_shapes=[pltpu.SMEM((8,), jnp.int32)],
        name="splat",
    )(point_target, positions.transpose(1, 0, 2), normals.transpose(1, 0, 2), weights)
    parts = resident(lax.all_to_all(parts, "scan", 0, 0, tiled=True))
    fields = resident(
        pl.pallas_call(
            combine_kernel,
            out_shape=shape(BLOCKS + 1, 8, 128),
            in_specs=vmem(2),
            out_specs=vmem(1)[0],
            name="combine",
        )(parts, resident(neighbours))
    )
    first, second, sums = pl.pallas_call(
        image_kernel,
        out_shape=(shape(BLOCKS, 8, 128), shape(BLOCKS, 8, 128), shape(128, 128)),
        in_specs=vmem(6),
        out_specs=tuple(vmem(3)),
        scratch_shapes=[
            pltpu.VMEM((5 * BLOCKS + 1, 8, 128), jnp.float32),
            pltpu.VMEM((5 * BLOCKS + 1, 8, 128), jnp.float32),
            pltpu.VMEM((3 * BLOCKS, 8, 128), jnp.float32),
            pltpu.VMEM((3 * BLOCKS, 128), jnp.int32),
            pltpu.SMEM((3 * BLOCKS, 128), jnp.int32),
            pltpu.VMEM((3 * BLOCKS * 32, 256), jnp.bfloat16),
            pltpu.SemaphoreType.DMA,
        ],
        name="images",
    )(fields, *around(fields), table)
    sums = resident(lax.all_to_all(sums, BOTH, 0, 0, tiled=True))
    return pl.pallas_call(
        last_kernel,
        out_shape=(jax.ShapeDtypeStruct((BLOCKS, 512), jnp.float32),) * 2,
        in_specs=vmem(4),
        out_specs=tuple(vmem(2)),
        scratch_shapes=[pltpu.VMEM((BLOCKS, 8, 128), jnp.float32)] * 2,
        name="last",
    )(sums, fields, resident(first), resident(second))


def solution(mesh):
    placed = (
        P(BOTH, None, None),
        P(BOTH, None, None),
        P(BOTH, None),
        P(BOTH),
        P(BOTH, None),
    )
    return jax.shard_map(
        per_device,
        mesh=mesh,
        in_specs=placed,
        out_specs=(P(BOTH, None), P(BOTH, None)),
        check_vma=False,
    )
```

```python
import jax
import jax.numpy as jnp
import numpy as np
from jax import lax
from jax.experimental import pallas as pl
from jax.experimental.pallas import tpu as pltpu
from jax.sharding import Mesh
from jax.sharding import PartitionSpec as P

SCREEN = 16.0
BLOCKS = 8
SLOTS = 4
SHARE = SLOTS * 8 + 8
ALL = ("scan", "pair", "half")
WINDOW = 6 * BLOCKS


def plane_table():
    mass = {-1: 1.0, 0: 4.0, 1: 1.0}
    stiff = {-1: -1.0, 0: 2.0, 1: -1.0}
    side = {0: 1, 7: -1}
    table = np.zeros((256, 128), np.float32)
    for group in range(4):
        for row in range(64):
            b = side.get(row // 8) if group in (1, 3) else 0
            c = side.get(row % 8) if group in (2, 3) else 0
            if b is None or c is None:
                continue
            for col in range(64):
                dj = 8 * b + row // 8 - col // 8
                dk = 8 * c + row % 8 - col % 8
                if abs(dj) <= 1 and abs(dk) <= 1:
                    table[64 * group + row, col] = mass[dj] * mass[dk]
                    table[64 * group + row, 64 + col] = stiff[dj] * mass[dk] + mass[dj] * stiff[dk]
    return table


def split(values):
    high = values.astype(jnp.bfloat16)
    low = (values - high.astype(jnp.float32)).astype(jnp.bfloat16)
    return high, low


def nt(left, right):
    return lax.dot_general(left, right, (((1,), (1,)), ((), ())), preferred_element_type=jnp.float32)


def left_half():
    return lax.broadcasted_iota(jnp.int32, (8, 128), 1) < 64


def splat_kernel(target_ref, spots_ref, norms_ref, weights_ref, near_ref, out_ref, used_ref, wide_ref):
    node = lax.broadcasted_iota(jnp.int32, (8, 128), 0).astype(jnp.float32)
    first_half = left_half()
    nothing = jnp.zeros((64, 128), jnp.float32)
    wide_ref[...] = jnp.full((8, 128), -1.0, jnp.float32)
    wide_ref[:, 0:27] = near_ref[...].astype(jnp.float32)
    names = jnp.where(first_half, -1.0, pltpu.roll(wide_ref[...], 64, 1))
    for row in range(8):
        used_ref[row] = 0
        for half in range(2):
            end = (2 * row + half + 1) * SHARE
            out_ref[end - 8 : end, :] = names
    for q in range(16):
        hats, slopes = [], []
        for dim in range(3):
            diff = spots_ref[dim, q : q + 1, :] - node
            dist = jnp.abs(diff)
            hats.append(jnp.maximum(0.0, 1.0 - dist))
            way = jnp.where(diff > 0.0, -1.0, jnp.where(diff < 0.0, 1.0, 0.0))
            slopes.append(jnp.where(dist < 1.0, way, 0.0))
        weight = weights_ref[q : q + 1, :]
        one = weight * norms_ref[0, q : q + 1, :] * slopes[0]
        two = weight * hats[0]
        three = SCREEN * two * hats[0]
        slope1 = norms_ref[1, q : q + 1, :] * slopes[1]
        slope2 = norms_ref[2, q : q + 1, :] * slopes[2]
        square1 = hats[1] * hats[1]
        square2 = hats[2] * hats[2]
        first = jnp.concatenate([hats[1][j : j + 1] * hats[2] for j in range(8)], axis=0)
        second = jnp.concatenate(
            [slope1[j : j + 1] * hats[2] + hats[1][j : j + 1] * slope2 for j in range(8)], axis=0
        )
        outer = jnp.concatenate([square1[j : j + 1] * square2 for j in range(8)], axis=0)
        right = jnp.concatenate(
            [jnp.concatenate([first, second], axis=1), jnp.concatenate([outer, nothing], axis=1)], axis=0
        )
        left = jnp.concatenate(
            [
                jnp.concatenate([one, two], axis=1),
                jnp.concatenate([three, jnp.zeros((8, 128), jnp.float32)], axis=1),
            ],
            axis=0,
        )
        right_high, right_low = split(right)
        left_high, left_low = split(left)
        main = nt(jnp.concatenate([left_high, left_low], axis=0), right_high)
        total = main[:16] + main[16:] + nt(left_high, right_low)
        target = target_ref[q]
        row = target // (16 * BLOCKS)
        slot = used_ref[row]
        used_ref[row] = slot + 1
        part = jnp.where(first_half, total[:8], total[8:])
        block = (target % BLOCKS).astype(jnp.float32)
        for half in range(2):
            share = (2 * row + half) * SHARE
            out_ref[pl.ds(pl.multiple_of(share + slot * 8, 8), 8), :] = part
            out_ref[pl.ds(share + SLOTS * 8 + slot, 1), 0:64] = jnp.full((1, 64), block, jnp.float32)


def local_names(table, base):
    named = table.astype(jnp.int32)
    local = named - base
    return jnp.where((named >= 0) & (local >= 0) & (local < WINDOW), local, WINDOW)


def window_base():
    pair = lax.axis_index("scan") * lax.axis_size("pair") + lax.axis_index("pair")
    return (2 * pair - 2) * BLOCKS


def combine_kernel(parts_ref, fields_ref, names_ref, full_ref, edge_ref):
    first_half = left_half()
    sums = [[jnp.zeros((8, 128), jnp.float32) for _ in range(BLOCKS)] for _ in range(2)]
    for source in range(16):
        at = source * SHARE
        tile = doubled(parts_ref[at + SLOTS * 8 : at + SLOTS * 8 + 8, :], first_half)
        into = sums[source % 2]
        for slot in range(SLOTS):
            part = parts_ref[at + slot * 8 : at + slot * 8 + 8, :]
            name = jnp.broadcast_to(tile[slot : slot + 1, :], (8, 128))
            for block in range(BLOCKS):
                into[block] = into[block] + jnp.where(name == float(block), part, 0.0)
    late = lax.axis_index("half") == 1
    row = 2 * lax.axis_index("scan")
    tables = []
    for half in range(2):
        at = pl.multiple_of((row + half) * SHARE + SLOTS * 8, 8)
        tables.append(pltpu.roll(parts_ref[pl.ds(at, 8), :], 64, 1))
        names_ref[half * BLOCKS : half * BLOCKS + BLOCKS, :] = local_names(tables[half], window_base())
    rest = []
    for block in range(BLOCKS):
        one, two = sums[0][block], sums[1][block]
        fields_ref[block] = one
        fields_ref[BLOCKS + block] = two
        full_ref[block] = jnp.where(late, two, one)
        rest.append(jnp.where(late, one, two))
    full_ref[BLOCKS] = jnp.where(late, tables[1], tables[0])
    for block in range(BLOCKS // 2):
        tile = jnp.where(first_half, rest[block], pltpu.roll(rest[block + BLOCKS // 2], 64, 1))
        full_ref[BLOCKS + 1 + block] = tile
        edge_ref[block] = tile


def doubled(tile, first_half):
    return jnp.where(first_half, tile, pltpu.roll(tile, 64, 1))


def couple(lookup, blocks, wide_ref, rows_ref, table_ref):
    lane = lax.broadcasted_iota(jnp.int32, (8, 128), 1)
    sublane = lax.broadcasted_iota(jnp.int32, (8, 128), 0)
    first_half = lane < 64
    low_j = lane % 64 < 32
    low_k = lane % 8 < 4
    top = sublane == 0
    bottom = sublane == 7

    def tiles(block, shift):
        def plane(b, c):
            return wide_ref[lookup(block, shift + 3 * (b + 1) + c + 1)]

        one = jnp.where(first_half, plane(0, 0), jnp.where(low_j, plane(1, 0), plane(-1, 0)))
        edges = jnp.where(low_k, plane(0, 1), plane(0, -1))
        corners = jnp.where(
            low_j,
            jnp.where(low_k, plane(1, 1), plane(1, -1)),
            jnp.where(low_k, plane(-1, 1), plane(-1, -1)),
        )
        return one, jnp.where(first_half, edges, corners)

    for block in range(blocks):
        before = tiles(block, 0)
        here = tiles(block, 9)
        after = tiles(block, 18)
        ends = [jnp.where(top, late, early) for early, late in zip(before, after)]
        rows = jnp.concatenate(
            [jnp.concatenate([here[half], ends[half]], axis=0) for half in range(2)], axis=1
        )
        high, low = split(rows)
        rows_ref[16 * block : 16 * block + 16, :] = high
        rows_ref[16 * (blocks + block) : 16 * (blocks + block) + 16, :] = low
    both = jnp.dot(rows_ref[0 : 32 * blocks, :], table_ref[...], preferred_element_type=jnp.float32)
    centre = jnp.where(first_half, 2.0 / 36.0, 4.0 / 36.0)
    side = jnp.where(first_half, -1.0 / 36.0, 1.0 / 36.0)
    result = []
    for block in range(blocks):
        at, other = 16 * block, 16 * (blocks + block)
        here = both[at : at + 8] + both[other : other + 8]
        ends = both[at + 8 : at + 16] + both[other + 8 : other + 16]
        before = pltpu.roll(jnp.where(bottom, ends, here), 1, 0)
        after = pltpu.roll(jnp.where(top, ends, here), 7, 0)
        value = centre * here + side * (before + after)
        result.append(value + pltpu.roll(value, 64, 1))
    return result


def total(lefts, rights, first_half):
    terms = [a * b for a, b in zip(lefts, rights)]
    while len(terms) > 1:
        terms = [a + b for a, b in zip(terms[::2], terms[1::2])]
    return jnp.sum(jnp.where(first_half, terms[0], 0.0), axis=(0, 1), keepdims=True)


def image_kernel(
    pair_ref,
    fields_ref,
    full_ref,
    edge_ref,
    table_ref,
    first_ref,
    second_ref,
    sums_ref,
    wide_ref,
    next_ref,
    screen_ref,
    index_ref,
    names_ref,
    other_ref,
    rows_ref,
    pair_done_ref,
    done_ref,
):
    first_half = left_half()
    half = lax.axis_index("half")
    pair_copy = pltpu.make_async_copy(pair_ref, index_ref, pair_done_ref)
    pair_copy.start()
    names_ref[...] = local_names(full_ref[BLOCKS], window_base())
    copy = pltpu.make_async_copy(names_ref, other_ref, done_ref)
    copy.start()
    beside = (1 + 3 * half) * BLOCKS
    packed = 5 * half * BLOCKS
    across = (4 - 3 * half) * BLOCKS
    for block in range(2 * BLOCKS):
        tile = fields_ref[block]
        turned = pltpu.roll(tile, 64, 1)
        wide_ref[2 * BLOCKS + block] = jnp.where(first_half, tile, turned)
        screen_ref[block] = jnp.where(first_half, turned, tile)
    for block in range(BLOCKS):
        tile = full_ref[block]
        turned = pltpu.roll(tile, 64, 1)
        wide_ref[beside + block] = jnp.where(first_half, tile, turned)
        screen_ref[2 * BLOCKS + block] = jnp.where(first_half, turned, tile)
    for block in range(BLOCKS // 2):
        for tile, place in ((full_ref[BLOCKS + 1 + block], packed), (edge_ref[block], across)):
            turned = pltpu.roll(tile, 64, 1)
            wide_ref[place + block] = jnp.where(first_half, tile, turned)
            wide_ref[place + BLOCKS // 2 + block] = jnp.where(first_half, turned, tile)
    nothing = jnp.zeros((8, 128), jnp.float32)
    wide_ref[WINDOW] = nothing
    next_ref[WINDOW] = nothing
    pair_copy.wait()
    copy.wait()

    def near(block, offset):
        if block < 2 * BLOCKS:
            return index_ref[block, offset]
        return other_ref[block - 2 * BLOCKS, offset]

    coupled = couple(near, 3 * BLOCKS, wide_ref, rows_ref, table_ref)
    for block in range(3 * BLOCKS):
        at = 2 * BLOCKS + block if block < 2 * BLOCKS else beside + block - 2 * BLOCKS
        next_ref[at] = screen_ref[block] * wide_ref[at] + coupled[block]
    own = (2 + half) * BLOCKS
    start = [wide_ref[own + block] for block in range(BLOCKS)]
    first = [next_ref[own + block] for block in range(BLOCKS)]

    def here(block, offset):
        return index_ref[half * BLOCKS + block, offset]

    coupled = couple(here, BLOCKS, next_ref, rows_ref, table_ref)
    second = []
    for block in range(BLOCKS):
        second.append(screen_ref[half * BLOCKS + block] * first[block] + coupled[block])
        first_ref[block] = first[block]
        second_ref[block] = second[block]
    lane = lax.broadcasted_iota(jnp.int32, (1, 128), 1)
    line = jnp.zeros((1, 128), jnp.float32)
    pairs = ((start, start), (start, first), (first, first), (start, second), (first, second))
    for place, (a, b) in enumerate(pairs):
        line = jnp.where(lane == place, total(a, b, first_half), line)
    sums_ref[...] = jnp.broadcast_to(line, (128, 128))


def last_kernel(sums_ref, fields_ref, first_ref, second_ref, solution_ref, residual_ref, left_ref, right_ref):
    first_half = left_half()
    sums = jnp.sum(sums_ref[...], axis=0, keepdims=True)
    lane = lax.broadcasted_iota(jnp.int32, (1, 128), 1)

    def pick(place):
        return jnp.sum(jnp.where(lane == place, sums, 0.0), axis=1, keepdims=True)

    s00, s01, s11, s02, s12 = (pick(place) for place in range(5))
    alpha0 = s00 / s01
    norm1 = s00 - 2.0 * alpha0 * s01 + alpha0 * alpha0 * s11
    beta = norm1 / s00
    grow = 1.0 + beta
    curve = grow * grow * s01 - grow * alpha0 * (s02 + s11) + alpha0 * alpha0 * s12
    alpha1 = norm1 / curve
    for block in range(BLOCKS):
        start = doubled(fields_ref[lax.axis_index("half") * BLOCKS + block], first_half)
        first = first_ref[block]
        left = start - alpha0 * first
        direction = left + beta * start
        image = grow * first - alpha0 * second_ref[block]
        left_ref[block] = alpha0 * start + alpha1 * direction
        right_ref[block] = left - alpha1 * image
    for pair in range(4):
        lanes = slice(128 * pair, 128 * pair + 128)
        solution_ref[:, lanes] = jnp.where(first_half, left_ref[:, 2 * pair, :], left_ref[:, 2 * pair + 1, :])
        residual_ref[:, lanes] = jnp.where(first_half, right_ref[:, 2 * pair, :], right_ref[:, 2 * pair + 1, :])


def vmem(count):
    return [pl.BlockSpec(memory_space=pltpu.VMEM)] * count


def smem(count):
    return [pl.BlockSpec(memory_space=pltpu.SMEM)] * count


def shape(*dims):
    return pltpu.VMEM(dims, jnp.float32)


def resident(values):
    return pltpu.with_memory_space_constraint(values, pltpu.VMEM)


def exchange(values, partners):
    return resident(lax.ppermute(values, ALL, list(enumerate(partners))))


def per_device(positions, normals, weights, point_target, neighbours):
    table = resident(jnp.asarray(plane_table(), jnp.bfloat16))
    parts = pl.pallas_call(
        splat_kernel,
        out_shape=shape(16 * SHARE, 128),
        in_specs=smem(1) + vmem(4),
        out_specs=vmem(1)[0],
        scratch_shapes=[pltpu.SMEM((8,), jnp.int32), pltpu.VMEM((8, 128), jnp.float32)],
        name="splat",
    )(point_target, positions.transpose(1, 0, 2), normals.transpose(1, 0, 2), weights, neighbours)
    parts = resident(lax.all_to_all(parts, ("scan", "half"), 0, 0, tiled=True))
    fields, names, full, edge = pl.pallas_call(
        combine_kernel,
        out_shape=(
            shape(2 * BLOCKS, 8, 128),
            pltpu.VMEM((2 * BLOCKS, 128), jnp.int32),
            shape(BLOCKS + 1 + BLOCKS // 2, 8, 128),
            shape(BLOCKS // 2, 8, 128),
        ),
        in_specs=vmem(1),
        out_specs=tuple(vmem(4)),
        name="combine",
    )(parts)
    fields = resident(fields)
    count = lax.axis_size("scan") * lax.axis_size("pair") * 2
    full = exchange(full, [(i - 1 + 2 * (i % 2)) % count for i in range(count)])
    edge = exchange(edge, [(i + 3 - 6 * (i % 2)) % count for i in range(count)])
    first, second, sums = pl.pallas_call(
        image_kernel,
        out_shape=(shape(BLOCKS, 8, 128), shape(BLOCKS, 8, 128), shape(128, 128)),
        in_specs=vmem(5),
        out_specs=tuple(vmem(3)),
        scratch_shapes=[
            pltpu.VMEM((WINDOW + 1, 8, 128), jnp.float32),
            pltpu.VMEM((WINDOW + 1, 8, 128), jnp.float32),
            pltpu.VMEM((3 * BLOCKS, 8, 128), jnp.float32),
            pltpu.SMEM((2 * BLOCKS, 128), jnp.int32),
            pltpu.VMEM((BLOCKS, 128), jnp.int32),
            pltpu.SMEM((BLOCKS, 128), jnp.int32),
            pltpu.VMEM((3 * BLOCKS * 32, 256), jnp.bfloat16),
            pltpu.SemaphoreType.DMA,
            pltpu.SemaphoreType.DMA,
        ],
        name="images",
    )(resident(names), fields, full, edge, table)
    sums = resident(lax.all_to_all(sums, ALL, 0, 0, tiled=True))
    return pl.pallas_call(
        last_kernel,
        out_shape=(jax.ShapeDtypeStruct((BLOCKS, 512), jnp.float32),) * 2,
        in_specs=vmem(4),
        out_specs=tuple(vmem(2)),
        scratch_shapes=[pltpu.VMEM((BLOCKS, 8, 128), jnp.float32)] * 2,
        name="last",
    )(sums, fields, resident(first), resident(second))


def solution(mesh):
    scan, morton = mesh.devices.shape
    paired = Mesh(mesh.devices.reshape(scan, morton // 2, 2), ALL)
    placed = (P(ALL, None, None), P(ALL, None, None), P(ALL, None), P(ALL), P(ALL, None))
    return jax.shard_map(
        per_device,
        mesh=paired,
        in_specs=placed,
        out_specs=(P(ALL, None), P(ALL, None)),
        check_vma=False,
    )
```

```python
import jax
import jax.numpy as jnp
import numpy as np
from jax import lax
from jax.experimental import pallas as pl
from jax.experimental.pallas import tpu as pltpu
from jax.sharding import Mesh
from jax.sharding import PartitionSpec as P

SCREEN = 16.0
BLOCKS = 8
SLOTS = 4
SHARE = SLOTS * 8 + 8
ALL = ("scan", "quad", "place")
WINDOW = 8 * BLOCKS


def plane_table():
    mass = {-1: 1.0, 0: 4.0, 1: 1.0}
    stiff = {-1: -1.0, 0: 2.0, 1: -1.0}
    side = {0: 1, 7: -1}
    table = np.zeros((256, 128), np.float32)
    for group in range(4):
        for row in range(64):
            b = side.get(row // 8) if group in (1, 3) else 0
            c = side.get(row % 8) if group in (2, 3) else 0
            if b is None or c is None:
                continue
            for col in range(64):
                dj = 8 * b + row // 8 - col // 8
                dk = 8 * c + row % 8 - col % 8
                if abs(dj) <= 1 and abs(dk) <= 1:
                    table[64 * group + row, col] = mass[dj] * mass[dk]
                    table[64 * group + row, 64 + col] = stiff[dj] * mass[dk] + mass[dj] * stiff[dk]
    return table


def split(values):
    high = values.astype(jnp.bfloat16)
    low = (values - high.astype(jnp.float32)).astype(jnp.bfloat16)
    return high, low


def nt(left, right):
    return lax.dot_general(left, right, (((1,), (1,)), ((), ())), preferred_element_type=jnp.float32)


def left_half():
    return lax.broadcasted_iota(jnp.int32, (8, 128), 1) < 64


def splat_kernel(target_ref, spots_ref, norms_ref, weights_ref, out_ref, used_ref):
    node = lax.broadcasted_iota(jnp.int32, (8, 128), 0).astype(jnp.float32)
    first_half = left_half()
    nothing = jnp.zeros((64, 128), jnp.float32)
    for row in range(8):
        used_ref[row] = 0
        out_ref[row * SHARE + SLOTS * 8 : (row + 1) * SHARE, :] = jnp.full((8, 128), -1.0, jnp.float32)
    for q in range(16):
        hats, slopes = [], []
        for dim in range(3):
            diff = spots_ref[dim, q : q + 1, :] - node
            dist = jnp.abs(diff)
            hats.append(jnp.maximum(0.0, 1.0 - dist))
            way = jnp.where(diff > 0.0, -1.0, jnp.where(diff < 0.0, 1.0, 0.0))
            slopes.append(jnp.where(dist < 1.0, way, 0.0))
        weight = weights_ref[q : q + 1, :]
        one = weight * norms_ref[0, q : q + 1, :] * slopes[0]
        two = weight * hats[0]
        three = SCREEN * two * hats[0]
        slope1 = norms_ref[1, q : q + 1, :] * slopes[1]
        slope2 = norms_ref[2, q : q + 1, :] * slopes[2]
        square1 = hats[1] * hats[1]
        square2 = hats[2] * hats[2]
        first = jnp.concatenate([hats[1][j : j + 1] * hats[2] for j in range(8)], axis=0)
        second = jnp.concatenate(
            [slope1[j : j + 1] * hats[2] + hats[1][j : j + 1] * slope2 for j in range(8)], axis=0
        )
        outer = jnp.concatenate([square1[j : j + 1] * square2 for j in range(8)], axis=0)
        right = jnp.concatenate(
            [jnp.concatenate([first, second], axis=1), jnp.concatenate([outer, nothing], axis=1)], axis=0
        )
        left = jnp.concatenate(
            [
                jnp.concatenate([one, two], axis=1),
                jnp.concatenate([three, jnp.zeros((8, 128), jnp.float32)], axis=1),
            ],
            axis=0,
        )
        right_high, right_low = split(right)
        left_high, left_low = split(left)
        main = nt(jnp.concatenate([left_high, left_low], axis=0), right_high)
        total = main[:16] + main[16:] + nt(left_high, right_low)
        target = target_ref[q]
        row = target // (16 * BLOCKS)
        slot = used_ref[row]
        used_ref[row] = slot + 1
        place = pl.multiple_of(row * SHARE + slot * 8, 8)
        out_ref[pl.ds(place, 8), :] = jnp.where(first_half, total[:8], total[8:])
        block = (target % BLOCKS).astype(jnp.float32)
        out_ref[pl.ds(row * SHARE + SLOTS * 8 + slot, 1), :] = jnp.full((1, 128), block, jnp.float32)


def local_names(table, base):
    named = table.astype(jnp.int32)
    local = named - base
    return jnp.where((named >= 0) & (local >= 0) & (local < WINDOW), 8 * local, 8 * WINDOW)


def window_base():
    quad = lax.axis_index("scan") * lax.axis_size("quad") + lax.axis_index("quad")
    return (4 * quad - 2) * BLOCKS


def combine_kernel(parts_ref, near_ref, out_ref):
    sums = [jnp.zeros((8, 128), jnp.float32) for _ in range(BLOCKS)]
    for source in range(8):
        for slot in range(SLOTS):
            at = source * SHARE
            part = parts_ref[at + slot * 8 : at + slot * 8 + 8, :]
            name = jnp.broadcast_to(parts_ref[at + SLOTS * 8 + slot : at + SLOTS * 8 + slot + 1, :], (8, 128))
            for block in range(BLOCKS):
                sums[block] = sums[block] + jnp.where(name == float(block), part, 0.0)
    for block in range(BLOCKS):
        out_ref[block] = sums[block]
    out_ref[BLOCKS] = jnp.full((8, 128), -1.0, jnp.float32)
    out_ref[BLOCKS, :, 0:27] = near_ref[...].astype(jnp.float32)


def pack_kernel(own_ref, beside_ref, out_ref):
    for block in range(BLOCKS):
        out_ref[block] = own_ref[block]
        out_ref[BLOCKS + block] = beside_ref[block]
    out_ref[2 * BLOCKS] = jnp.where(left_half(), own_ref[BLOCKS], pltpu.roll(beside_ref[BLOCKS], 64, 1))


def doubled(tile, first_half):
    return jnp.where(first_half, tile, pltpu.roll(tile, 64, 1))


def rows_at(first):
    return pl.ds(pl.multiple_of(first, 8), 8)


def tile_at(block):
    return rows_at(8 * block)


def couple(lookup, blocks, wide_ref, rows_ref, table_ref):
    lane = lax.broadcasted_iota(jnp.int32, (8, 128), 1)
    sublane = lax.broadcasted_iota(jnp.int32, (8, 128), 0)
    first_half = lane < 64
    low_j = lane % 64 < 32
    low_k = lane % 8 < 4
    top = sublane == 0
    bottom = sublane == 7

    def tiles(block, shift):
        def plane(b, c):
            return wide_ref[rows_at(lookup(block, shift + 3 * (b + 1) + c + 1)), :]

        one = jnp.where(first_half, plane(0, 0), jnp.where(low_j, plane(1, 0), plane(-1, 0)))
        edges = jnp.where(low_k, plane(0, 1), plane(0, -1))
        corners = jnp.where(
            low_j,
            jnp.where(low_k, plane(1, 1), plane(1, -1)),
            jnp.where(low_k, plane(-1, 1), plane(-1, -1)),
        )
        return one, jnp.where(first_half, edges, corners)

    for block in range(blocks):
        before = tiles(block, 0)
        here = tiles(block, 9)
        after = tiles(block, 18)
        ends = [jnp.where(top, late, early) for early, late in zip(before, after)]
        rows = jnp.concatenate(
            [jnp.concatenate([here[half], ends[half]], axis=0) for half in range(2)], axis=1
        )
        high, low = split(rows)
        rows_ref[16 * block : 16 * block + 16, :] = high
        rows_ref[16 * (blocks + block) : 16 * (blocks + block) + 16, :] = low
    both = jnp.dot(rows_ref[0 : 32 * blocks, :], table_ref[...], preferred_element_type=jnp.float32)
    centre = jnp.where(first_half, 2.0 / 36.0, 4.0 / 36.0)
    side = jnp.where(first_half, -1.0 / 36.0, 1.0 / 36.0)
    result = []
    for block in range(blocks):
        at, other = 16 * block, 16 * (blocks + block)
        here = both[at : at + 8] + both[other : other + 8]
        ends = both[at + 8 : at + 16] + both[other + 8 : other + 16]
        before = pltpu.roll(jnp.where(bottom, ends, here), 1, 0)
        after = pltpu.roll(jnp.where(top, ends, here), 7, 0)
        value = centre * here + side * (before + after)
        result.append(value + pltpu.roll(value, 64, 1))
    return result


def total(lefts, rights, first_half):
    terms = [a * b for a, b in zip(lefts, rights)]
    while len(terms) > 1:
        terms = [a + b for a, b in zip(terms[::2], terms[1::2])]
    return jnp.sum(jnp.where(first_half, terms[0], 0.0), axis=(0, 1), keepdims=True)


def image_kernel(
    own_ref,
    one_ref,
    two_ref,
    three_ref,
    table_ref,
    first_ref,
    second_ref,
    sums_ref,
    wide_ref,
    next_ref,
    screen_ref,
    names_ref,
    index_ref,
    rows_ref,
    done_ref,
):
    first_half = left_half()
    place = lax.axis_index("place")
    parts = []
    for step, ref in enumerate((own_ref, one_ref, two_ref, three_ref)):
        member = lax.bitwise_xor(place, step)
        parts.append((ref, (2 + member) * BLOCKS, lax.rem(member + 6, 8) * BLOCKS))
    for ref, inner, outer in parts:
        tile = ref[2 * BLOCKS]
        names_ref[pl.ds(pl.multiple_of(inner, 8), 8), :] = local_names(tile, window_base())
        names_ref[pl.ds(pl.multiple_of(outer, 8), 8), :] = local_names(pltpu.roll(tile, 64, 1), window_base())
    copy = pltpu.make_async_copy(names_ref.at[pl.ds(BLOCKS, 6 * BLOCKS)], index_ref, done_ref)
    copy.start()
    for ref, inner, outer in parts:
        for block in range(2 * BLOCKS):
            at = inner + block if block < BLOCKS else outer + block - BLOCKS
            tile = ref[block]
            turned = pltpu.roll(tile, 64, 1)
            wide_ref[tile_at(at), :] = jnp.where(first_half, tile, turned)
            screen_ref[tile_at(at), :] = jnp.where(first_half, turned, tile)
    nothing = jnp.zeros((8, 128), jnp.float32)
    wide_ref[tile_at(WINDOW), :] = nothing
    next_ref[tile_at(WINDOW), :] = nothing
    copy.wait()

    def near(block, offset):
        return index_ref[block, offset]

    def inside(block, offset):
        return index_ref[BLOCKS + block, offset]

    coupled = couple(near, 6 * BLOCKS, wide_ref, rows_ref, table_ref)
    for block in range(6 * BLOCKS):
        at = BLOCKS + block
        next_ref[tile_at(at), :] = screen_ref[tile_at(at), :] * wide_ref[tile_at(at), :] + coupled[block]
    start = [wide_ref[tile_at(2 * BLOCKS + block), :] for block in range(4 * BLOCKS)]
    first = [next_ref[tile_at(2 * BLOCKS + block), :] for block in range(4 * BLOCKS)]
    coupled = couple(inside, 4 * BLOCKS, next_ref, rows_ref, table_ref)
    second = []
    for block in range(4 * BLOCKS):
        image = screen_ref[tile_at(2 * BLOCKS + block), :] * first[block] + coupled[block]
        second.append(image)
        wide_ref[tile_at(block), :] = image
    for block in range(BLOCKS):
        first_ref[block] = next_ref[tile_at((2 + place) * BLOCKS + block), :]
        second_ref[block] = wide_ref[tile_at(place * BLOCKS + block), :]
    lane = lax.broadcasted_iota(jnp.int32, (1, 128), 1)
    line = jnp.zeros((1, 128), jnp.float32)
    pairs = ((start, start), (start, first), (first, first), (start, second), (first, second))
    for slot, (a, b) in enumerate(pairs):
        line = jnp.where(lane == slot, total(a, b, first_half), line)
    sums_ref[...] = jnp.broadcast_to(line, (32, 128))


def last_kernel(sums_ref, fields_ref, first_ref, second_ref, solution_ref, residual_ref, left_ref, right_ref):
    first_half = left_half()
    sums = jnp.sum(sums_ref[...], axis=0, keepdims=True)
    lane = lax.broadcasted_iota(jnp.int32, (1, 128), 1)

    def pick(place):
        return jnp.sum(jnp.where(lane == place, sums, 0.0), axis=1, keepdims=True)

    s00, s01, s11, s02, s12 = (pick(place) for place in range(5))
    alpha0 = s00 / s01
    norm1 = s00 - 2.0 * alpha0 * s01 + alpha0 * alpha0 * s11
    beta = norm1 / s00
    grow = 1.0 + beta
    curve = grow * grow * s01 - grow * alpha0 * (s02 + s11) + alpha0 * alpha0 * s12
    alpha1 = norm1 / curve
    for block in range(BLOCKS):
        start = doubled(fields_ref[block], first_half)
        first = first_ref[block]
        left = start - alpha0 * first
        direction = left + beta * start
        image = grow * first - alpha0 * second_ref[block]
        left_ref[block] = alpha0 * start + alpha1 * direction
        right_ref[block] = left - alpha1 * image
    for pair in range(4):
        lanes = slice(128 * pair, 128 * pair + 128)
        solution_ref[:, lanes] = jnp.where(first_half, left_ref[:, 2 * pair, :], left_ref[:, 2 * pair + 1, :])
        residual_ref[:, lanes] = jnp.where(first_half, right_ref[:, 2 * pair, :], right_ref[:, 2 * pair + 1, :])


def vmem(count):
    return [pl.BlockSpec(memory_space=pltpu.VMEM)] * count


def smem(count):
    return [pl.BlockSpec(memory_space=pltpu.SMEM)] * count


def shape(*dims):
    return pltpu.VMEM(dims, jnp.float32)


def resident(values):
    return pltpu.with_memory_space_constraint(values, pltpu.VMEM)


def per_device(positions, normals, weights, point_target, neighbours):
    table = resident(jnp.asarray(plane_table(), jnp.bfloat16))
    parts = pl.pallas_call(
        splat_kernel,
        out_shape=shape(8 * SHARE, 128),
        in_specs=smem(1) + vmem(3),
        out_specs=vmem(1)[0],
        scratch_shapes=[pltpu.SMEM((8,), jnp.int32)],
        name="splat",
    )(point_target, positions.transpose(1, 0, 2), normals.transpose(1, 0, 2), weights)
    parts = resident(lax.all_to_all(parts, "scan", 0, 0, tiled=True))
    fields = resident(
        pl.pallas_call(
            combine_kernel,
            out_shape=shape(BLOCKS + 1, 8, 128),
            in_specs=vmem(2),
            out_specs=vmem(1)[0],
            name="combine",
        )(parts, resident(neighbours))
    )
    count = lax.axis_size("scan") * lax.axis_size("quad") * 4
    beside = resident(lax.ppermute(fields, ALL, [(i, (i - 4 if i % 4 < 2 else i + 4) % count) for i in range(count)]))
    packed = resident(
        pl.pallas_call(
            pack_kernel,
            out_shape=shape(2 * BLOCKS + 1, 8, 128),
            in_specs=vmem(2),
            out_specs=vmem(1)[0],
            name="pack",
        )(fields, beside)
    )
    others = [resident(lax.ppermute(packed, "place", [(i, i ^ step) for i in range(4)])) for step in (1, 2, 3)]
    first, second, sums = pl.pallas_call(
        image_kernel,
        out_shape=(shape(BLOCKS, 8, 128), shape(BLOCKS, 8, 128), shape(32, 128)),
        in_specs=vmem(5),
        out_specs=tuple(vmem(3)),
        scratch_shapes=[
            pltpu.VMEM((8 * WINDOW + 8, 128), jnp.float32),
            pltpu.VMEM((8 * WINDOW + 8, 128), jnp.float32),
            pltpu.VMEM((8 * WINDOW, 128), jnp.float32),
            pltpu.VMEM((WINDOW, 128), jnp.int32),
            pltpu.SMEM((6 * BLOCKS, 128), jnp.int32),
            pltpu.VMEM((6 * BLOCKS * 32, 256), jnp.bfloat16),
            pltpu.SemaphoreType.DMA,
        ],
        name="images",
    )(packed, *others, table)
    sums = resident(lax.all_to_all(sums, ("scan", "quad"), 0, 0, tiled=True))
    return pl.pallas_call(
        last_kernel,
        out_shape=(jax.ShapeDtypeStruct((BLOCKS, 512), jnp.float32),) * 2,
        in_specs=vmem(4),
        out_specs=tuple(vmem(2)),
        scratch_shapes=[pltpu.VMEM((BLOCKS, 8, 128), jnp.float32)] * 2,
        name="last",
    )(sums, fields, resident(first), resident(second))


def solution(mesh):
    scan, morton = mesh.devices.shape
    grouped = Mesh(mesh.devices.reshape(scan, morton // 4, 4), ALL)
    placed = (P(ALL, None, None), P(ALL, None, None), P(ALL, None), P(ALL), P(ALL, None))
    return jax.shard_map(
        per_device,
        mesh=grouped,
        in_specs=placed,
        out_specs=(P(ALL, None), P(ALL, None)),
        check_vma=False,
    )
```

```python
import jax
import jax.numpy as jnp
import numpy as np
from jax import lax
from jax.experimental import pallas as pl
from jax.experimental.pallas import tpu as pltpu
from jax.sharding import Mesh
from jax.sharding import PartitionSpec as P

SCREEN = 16.0
BLOCKS = 8
SLOTS = 4
SHARE = SLOTS * 8 + 8
ALL = ("scan", "quad", "place")
WINDOW = 8 * BLOCKS


def plane_table():
    mass = {-1: 1.0, 0: 4.0, 1: 1.0}
    stiff = {-1: -1.0, 0: 2.0, 1: -1.0}
    side = {0: 1, 7: -1}
    table = np.zeros((256, 128), np.float32)
    for group in range(4):
        for row in range(64):
            b = side.get(row // 8) if group in (1, 3) else 0
            c = side.get(row % 8) if group in (2, 3) else 0
            if b is None or c is None:
                continue
            for col in range(64):
                dj = 8 * b + row // 8 - col // 8
                dk = 8 * c + row % 8 - col % 8
                if abs(dj) <= 1 and abs(dk) <= 1:
                    table[64 * group + row, col] = mass[dj] * mass[dk]
                    table[64 * group + row, 64 + col] = stiff[dj] * mass[dk] + mass[dj] * stiff[dk]
    return table


def split(values):
    high = values.astype(jnp.bfloat16)
    low = (values - high.astype(jnp.float32)).astype(jnp.bfloat16)
    return high, low


def nt(left, right):
    return lax.dot_general(left, right, (((1,), (1,)), ((), ())), preferred_element_type=jnp.float32)


def left_half():
    return lax.broadcasted_iota(jnp.int32, (8, 128), 1) < 64


def splat_kernel(target_ref, spots_ref, norms_ref, weights_ref, out_ref, used_ref):
    node = lax.broadcasted_iota(jnp.int32, (8, 128), 0).astype(jnp.float32)
    first_half = left_half()
    nothing = jnp.zeros((64, 128), jnp.float32)
    for row in range(8):
        used_ref[row] = 0
        out_ref[row * SHARE + SLOTS * 8 : (row + 1) * SHARE, :] = jnp.full((8, 128), -1.0, jnp.float32)
    for q in range(16):
        hats, slopes = [], []
        for dim in range(3):
            diff = spots_ref[dim, q : q + 1, :] - node
            dist = jnp.abs(diff)
            hats.append(jnp.maximum(0.0, 1.0 - dist))
            way = jnp.where(diff > 0.0, -1.0, jnp.where(diff < 0.0, 1.0, 0.0))
            slopes.append(jnp.where(dist < 1.0, way, 0.0))
        weight = weights_ref[q : q + 1, :]
        one = weight * norms_ref[0, q : q + 1, :] * slopes[0]
        two = weight * hats[0]
        three = SCREEN * two * hats[0]
        slope1 = norms_ref[1, q : q + 1, :] * slopes[1]
        slope2 = norms_ref[2, q : q + 1, :] * slopes[2]
        square1 = hats[1] * hats[1]
        square2 = hats[2] * hats[2]
        first = jnp.concatenate([hats[1][j : j + 1] * hats[2] for j in range(8)], axis=0)
        second = jnp.concatenate(
            [slope1[j : j + 1] * hats[2] + hats[1][j : j + 1] * slope2 for j in range(8)], axis=0
        )
        outer = jnp.concatenate([square1[j : j + 1] * square2 for j in range(8)], axis=0)
        right = jnp.concatenate(
            [jnp.concatenate([first, second], axis=1), jnp.concatenate([outer, nothing], axis=1)], axis=0
        )
        left = jnp.concatenate(
            [
                jnp.concatenate([one, two], axis=1),
                jnp.concatenate([three, jnp.zeros((8, 128), jnp.float32)], axis=1),
            ],
            axis=0,
        )
        right_high, right_low = split(right)
        left_high, left_low = split(left)
        main = nt(jnp.concatenate([left_high, left_low], axis=0), right_high)
        total = main[:16] + main[16:] + nt(left_high, right_low)
        target = target_ref[q]
        row = target // (16 * BLOCKS)
        slot = used_ref[row]
        used_ref[row] = slot + 1
        place = pl.multiple_of(row * SHARE + slot * 8, 8)
        out_ref[pl.ds(place, 8), :] = jnp.where(first_half, total[:8], total[8:])
        block = (target % BLOCKS).astype(jnp.float32)
        out_ref[pl.ds(row * SHARE + SLOTS * 8 + slot, 1), :] = jnp.full((1, 128), block, jnp.float32)


def local_names(table, base):
    named = table.astype(jnp.int32)
    local = named - base
    return jnp.where((named >= 0) & (local >= 0) & (local < WINDOW), 8 * local, 8 * WINDOW)


def window_base():
    quad = lax.axis_index("scan") * lax.axis_size("quad") + lax.axis_index("quad")
    return (4 * quad - 2) * BLOCKS


def combine_kernel(parts_ref, near_ref, out_ref):
    sums = [jnp.zeros((8, 128), jnp.float32) for _ in range(BLOCKS)]
    for source in range(8):
        for slot in range(SLOTS):
            at = source * SHARE
            part = parts_ref[at + slot * 8 : at + slot * 8 + 8, :]
            name = jnp.broadcast_to(parts_ref[at + SLOTS * 8 + slot : at + SLOTS * 8 + slot + 1, :], (8, 128))
            for block in range(BLOCKS):
                sums[block] = sums[block] + jnp.where(name == float(block), part, 0.0)
    for block in range(BLOCKS):
        out_ref[block] = sums[block]
    out_ref[BLOCKS] = jnp.full((8, 128), -1.0, jnp.float32)
    out_ref[BLOCKS, :, 0:27] = near_ref[...].astype(jnp.float32)


def pack_kernel(own_ref, beside_ref, out_ref):
    for block in range(BLOCKS):
        out_ref[block] = own_ref[block]
        out_ref[BLOCKS + block] = beside_ref[block]
    out_ref[2 * BLOCKS] = jnp.where(left_half(), own_ref[BLOCKS], pltpu.roll(beside_ref[BLOCKS], 64, 1))


def doubled(tile, first_half):
    return jnp.where(first_half, tile, pltpu.roll(tile, 64, 1))


def rows_at(first):
    return pl.ds(pl.multiple_of(first, 8), 8)


def tile_at(block):
    return rows_at(8 * block)


def couple(lookup, blocks, wide_ref, rows_ref, table_ref):
    lane = lax.broadcasted_iota(jnp.int32, (8, 128), 1)
    sublane = lax.broadcasted_iota(jnp.int32, (8, 128), 0)
    first_half = lane < 64
    low_j = lane % 64 < 32
    low_k = lane % 8 < 4
    top = sublane == 0
    bottom = sublane == 7

    def tiles(block, shift):
        def plane(b, c):
            return wide_ref[rows_at(lookup(block, shift + 3 * (b + 1) + c + 1)), :]

        one = jnp.where(first_half, plane(0, 0), jnp.where(low_j, plane(1, 0), plane(-1, 0)))
        edges = jnp.where(low_k, plane(0, 1), plane(0, -1))
        corners = jnp.where(
            low_j,
            jnp.where(low_k, plane(1, 1), plane(1, -1)),
            jnp.where(low_k, plane(-1, 1), plane(-1, -1)),
        )
        return one, jnp.where(first_half, edges, corners)

    for block in range(blocks):
        before = tiles(block, 0)
        here = tiles(block, 9)
        after = tiles(block, 18)
        ends = [jnp.where(top, late, early) for early, late in zip(before, after)]
        rows = jnp.concatenate(
            [jnp.concatenate([here[half], ends[half]], axis=0) for half in range(2)], axis=1
        )
        high, low = split(rows)
        rows_ref[16 * block : 16 * block + 16, :] = high
        rows_ref[16 * (blocks + block) : 16 * (blocks + block) + 16, :] = low
    both = jnp.dot(rows_ref[0 : 32 * blocks, :], table_ref[...], preferred_element_type=jnp.float32)
    centre = jnp.where(first_half, 2.0 / 36.0, 4.0 / 36.0)
    side = jnp.where(first_half, -1.0 / 36.0, 1.0 / 36.0)
    result = []
    for block in range(blocks):
        at, other = 16 * block, 16 * (blocks + block)
        here = both[at : at + 8] + both[other : other + 8]
        ends = both[at + 8 : at + 16] + both[other + 8 : other + 16]
        before = pltpu.roll(jnp.where(bottom, ends, here), 1, 0)
        after = pltpu.roll(jnp.where(top, ends, here), 7, 0)
        value = centre * here + side * (before + after)
        result.append(value + pltpu.roll(value, 64, 1))
    return result


def total(lefts, rights, first_half):
    terms = [a * b for a, b in zip(lefts, rights)]
    while len(terms) > 1:
        terms = [a + b for a, b in zip(terms[::2], terms[1::2])]
    return jnp.sum(jnp.where(first_half, terms[0], 0.0), axis=(0, 1), keepdims=True)


def image_kernel(
    own_ref,
    one_ref,
    two_ref,
    three_ref,
    table_ref,
    first_ref,
    second_ref,
    sums_ref,
    wide_ref,
    next_ref,
    screen_ref,
    names_ref,
    short_ref,
    index_ref,
    rows_ref,
    done_ref,
):
    first_half = left_half()
    place = lax.axis_index("place")
    parts = []
    for step, ref in enumerate((own_ref, one_ref, two_ref, three_ref)):
        member = lax.bitwise_xor(place, step)
        parts.append((ref, (2 + member) * BLOCKS, lax.rem(member + 6, 8) * BLOCKS))
    for ref, inner, outer in parts:
        tile = ref[2 * BLOCKS]
        names_ref[pl.ds(pl.multiple_of(inner, 8), 8), :] = local_names(tile, window_base())
        names_ref[pl.ds(pl.multiple_of(outer, 8), 8), :] = local_names(pltpu.roll(tile, 64, 1), window_base())
    group = lax.broadcasted_iota(jnp.int32, (8, 128), 1) // 32
    for half, members in ((0, (1, 2, 3, 4)), (1, (5, 6))):
        tile = names_ref[8 * members[0] : 8 * members[0] + 8, :]
        for slot, member in enumerate(members[1:], 1):
            other = pltpu.roll(names_ref[8 * member : 8 * member + 8, :], 32 * slot, 1)
            tile = jnp.where(group == slot, other, tile)
        short_ref[8 * half : 8 * half + 8, :] = tile
    copy = pltpu.make_async_copy(short_ref, index_ref, done_ref)
    copy.start()
    for ref, inner, outer in parts:
        for block in range(2 * BLOCKS):
            at = inner + block if block < BLOCKS else outer + block - BLOCKS
            tile = ref[block]
            turned = pltpu.roll(tile, 64, 1)
            wide_ref[tile_at(at), :] = jnp.where(first_half, tile, turned)
            screen_ref[tile_at(at), :] = jnp.where(first_half, turned, tile)
    nothing = jnp.zeros((8, 128), jnp.float32)
    wide_ref[tile_at(WINDOW), :] = nothing
    next_ref[tile_at(WINDOW), :] = nothing
    copy.wait()

    def near(block, offset):
        device = block // BLOCKS
        return index_ref[device // 4 * BLOCKS + block % BLOCKS, device % 4 * 32 + offset]

    def inside(block, offset):
        return near(BLOCKS + block, offset)

    coupled = couple(near, 6 * BLOCKS, wide_ref, rows_ref, table_ref)
    for block in range(6 * BLOCKS):
        at = BLOCKS + block
        next_ref[tile_at(at), :] = screen_ref[tile_at(at), :] * wide_ref[tile_at(at), :] + coupled[block]
    start = [wide_ref[tile_at(2 * BLOCKS + block), :] for block in range(4 * BLOCKS)]
    first = [next_ref[tile_at(2 * BLOCKS + block), :] for block in range(4 * BLOCKS)]
    coupled = couple(inside, 4 * BLOCKS, next_ref, rows_ref, table_ref)
    second = []
    for block in range(4 * BLOCKS):
        image = screen_ref[tile_at(2 * BLOCKS + block), :] * first[block] + coupled[block]
        second.append(image)
        wide_ref[tile_at(block), :] = image
    for block in range(BLOCKS):
        first_ref[block] = next_ref[tile_at((2 + place) * BLOCKS + block), :]
        second_ref[block] = wide_ref[tile_at(place * BLOCKS + block), :]
    lane = lax.broadcasted_iota(jnp.int32, (1, 128), 1)
    line = jnp.zeros((1, 128), jnp.float32)
    pairs = ((start, start), (start, first), (first, first), (start, second), (first, second))
    for slot, (a, b) in enumerate(pairs):
        line = jnp.where(lane == slot, total(a, b, first_half), line)
    sums_ref[...] = jnp.broadcast_to(line, (32, 128))


def last_kernel(sums_ref, fields_ref, first_ref, second_ref, solution_ref, residual_ref, left_ref, right_ref):
    first_half = left_half()
    sums = jnp.sum(sums_ref[...], axis=0, keepdims=True)
    lane = lax.broadcasted_iota(jnp.int32, (1, 128), 1)

    def pick(place):
        return jnp.sum(jnp.where(lane == place, sums, 0.0), axis=1, keepdims=True)

    s00, s01, s11, s02, s12 = (pick(place) for place in range(5))
    alpha0 = s00 / s01
    norm1 = s00 - 2.0 * alpha0 * s01 + alpha0 * alpha0 * s11
    beta = norm1 / s00
    grow = 1.0 + beta
    curve = grow * grow * s01 - grow * alpha0 * (s02 + s11) + alpha0 * alpha0 * s12
    alpha1 = norm1 / curve
    for block in range(BLOCKS):
        start = doubled(fields_ref[block], first_half)
        first = first_ref[block]
        left = start - alpha0 * first
        direction = left + beta * start
        image = grow * first - alpha0 * second_ref[block]
        left_ref[block] = alpha0 * start + alpha1 * direction
        right_ref[block] = left - alpha1 * image
    for pair in range(4):
        lanes = slice(128 * pair, 128 * pair + 128)
        solution_ref[:, lanes] = jnp.where(first_half, left_ref[:, 2 * pair, :], left_ref[:, 2 * pair + 1, :])
        residual_ref[:, lanes] = jnp.where(first_half, right_ref[:, 2 * pair, :], right_ref[:, 2 * pair + 1, :])


def vmem(count):
    return [pl.BlockSpec(memory_space=pltpu.VMEM)] * count


def smem(count):
    return [pl.BlockSpec(memory_space=pltpu.SMEM)] * count


def shape(*dims):
    return pltpu.VMEM(dims, jnp.float32)


def resident(values):
    return pltpu.with_memory_space_constraint(values, pltpu.VMEM)


def per_device(positions, normals, weights, point_target, neighbours):
    table = resident(jnp.asarray(plane_table(), jnp.bfloat16))
    parts = pl.pallas_call(
        splat_kernel,
        out_shape=shape(8 * SHARE, 128),
        in_specs=smem(1) + vmem(3),
        out_specs=vmem(1)[0],
        scratch_shapes=[pltpu.SMEM((8,), jnp.int32)],
        name="splat",
    )(point_target, positions.transpose(1, 0, 2), normals.transpose(1, 0, 2), weights)
    parts = resident(lax.all_to_all(parts, "scan", 0, 0, tiled=True))
    fields = resident(
        pl.pallas_call(
            combine_kernel,
            out_shape=shape(BLOCKS + 1, 8, 128),
            in_specs=vmem(2),
            out_specs=vmem(1)[0],
            name="combine",
        )(parts, resident(neighbours))
    )
    count = lax.axis_size("scan") * lax.axis_size("quad") * 4
    beside = resident(lax.ppermute(fields, ALL, [(i, (i - 4 if i % 4 < 2 else i + 4) % count) for i in range(count)]))
    packed = resident(
        pl.pallas_call(
            pack_kernel,
            out_shape=shape(2 * BLOCKS + 1, 8, 128),
            in_specs=vmem(2),
            out_specs=vmem(1)[0],
            name="pack",
        )(fields, beside)
    )
    others = [resident(lax.ppermute(packed, "place", [(i, i ^ step) for i in range(4)])) for step in (1, 2, 3)]
    first, second, sums = pl.pallas_call(
        image_kernel,
        out_shape=(shape(BLOCKS, 8, 128), shape(BLOCKS, 8, 128), shape(32, 128)),
        in_specs=vmem(5),
        out_specs=tuple(vmem(3)),
        scratch_shapes=[
            pltpu.VMEM((8 * WINDOW + 8, 128), jnp.float32),
            pltpu.VMEM((8 * WINDOW + 8, 128), jnp.float32),
            pltpu.VMEM((8 * WINDOW, 128), jnp.float32),
            pltpu.VMEM((WINDOW, 128), jnp.int32),
            pltpu.VMEM((2 * BLOCKS, 128), jnp.int32),
            pltpu.SMEM((2 * BLOCKS, 128), jnp.int32),
            pltpu.VMEM((6 * BLOCKS * 32, 256), jnp.bfloat16),
            pltpu.SemaphoreType.DMA,
        ],
        name="images",
    )(packed, *others, table)
    sums = resident(lax.all_to_all(sums, ("scan", "quad"), 0, 0, tiled=True))
    return pl.pallas_call(
        last_kernel,
        out_shape=(jax.ShapeDtypeStruct((BLOCKS, 512), jnp.float32),) * 2,
        in_specs=vmem(4),
        out_specs=tuple(vmem(2)),
        scratch_shapes=[pltpu.VMEM((BLOCKS, 8, 128), jnp.float32)] * 2,
        name="last",
    )(sums, fields, resident(first), resident(second))


def solution(mesh):
    scan, morton = mesh.devices.shape
    grouped = Mesh(mesh.devices.reshape(scan, morton // 4, 4), ALL)
    placed = (P(ALL, None, None), P(ALL, None, None), P(ALL, None), P(ALL), P(ALL, None))
    return jax.shard_map(
        per_device,
        mesh=grouped,
        in_specs=placed,
        out_specs=(P(ALL, None), P(ALL, None)),
        check_vma=False,
    )
```

```python
import jax
import jax.numpy as jnp
import numpy as np
from jax import lax
from jax.experimental import pallas as pl
from jax.experimental.pallas import tpu as pltpu
from jax.sharding import Mesh
from jax.sharding import PartitionSpec as P

SCREEN = 16.0
BLOCKS = 8
SLOTS = 4
SHARE = SLOTS * 8 + 8
ALL = ("scan", "quad", "place")
WINDOW = 8 * BLOCKS


def plane_table():
    mass = {-1: 1.0, 0: 4.0, 1: 1.0}
    stiff = {-1: -1.0, 0: 2.0, 1: -1.0}
    side = {0: 1, 7: -1}
    table = np.zeros((256, 128), np.float32)
    for group in range(4):
        for row in range(64):
            b = side.get(row // 8) if group in (1, 3) else 0
            c = side.get(row % 8) if group in (2, 3) else 0
            if b is None or c is None:
                continue
            for col in range(64):
                dj = 8 * b + row // 8 - col // 8
                dk = 8 * c + row % 8 - col % 8
                if abs(dj) <= 1 and abs(dk) <= 1:
                    table[64 * group + row, col] = mass[dj] * mass[dk]
                    table[64 * group + row, 64 + col] = stiff[dj] * mass[dk] + mass[dj] * stiff[dk]
    return table


def split(values):
    high = values.astype(jnp.bfloat16)
    low = (values - high.astype(jnp.float32)).astype(jnp.bfloat16)
    return high, low


def nt(left, right):
    return lax.dot_general(left, right, (((1,), (1,)), ((), ())), preferred_element_type=jnp.float32)


def left_half():
    return lax.broadcasted_iota(jnp.int32, (8, 128), 1) < 64


def splat_kernel(target_ref, spots_ref, norms_ref, weights_ref, out_ref, used_ref):
    node = lax.broadcasted_iota(jnp.int32, (8, 128), 0).astype(jnp.float32)
    first_half = left_half()
    nothing = jnp.zeros((64, 128), jnp.float32)
    for row in range(8):
        used_ref[row] = 0
        out_ref[row * SHARE + SLOTS * 8 : (row + 1) * SHARE, :] = jnp.full((8, 128), -1.0, jnp.float32)
    for q in range(16):
        hats, slopes = [], []
        for dim in range(3):
            diff = spots_ref[dim, q : q + 1, :] - node
            dist = jnp.abs(diff)
            hats.append(jnp.maximum(0.0, 1.0 - dist))
            way = jnp.where(diff > 0.0, -1.0, jnp.where(diff < 0.0, 1.0, 0.0))
            slopes.append(jnp.where(dist < 1.0, way, 0.0))
        weight = weights_ref[q : q + 1, :]
        one = weight * norms_ref[0, q : q + 1, :] * slopes[0]
        two = weight * hats[0]
        three = SCREEN * two * hats[0]
        slope1 = norms_ref[1, q : q + 1, :] * slopes[1]
        slope2 = norms_ref[2, q : q + 1, :] * slopes[2]
        square1 = hats[1] * hats[1]
        square2 = hats[2] * hats[2]
        first = jnp.concatenate([hats[1][j : j + 1] * hats[2] for j in range(8)], axis=0)
        second = jnp.concatenate(
            [slope1[j : j + 1] * hats[2] + hats[1][j : j + 1] * slope2 for j in range(8)], axis=0
        )
        outer = jnp.concatenate([square1[j : j + 1] * square2 for j in range(8)], axis=0)
        right = jnp.concatenate(
            [jnp.concatenate([first, second], axis=1), jnp.concatenate([outer, nothing], axis=1)], axis=0
        )
        left = jnp.concatenate(
            [
                jnp.concatenate([one, two], axis=1),
                jnp.concatenate([three, jnp.zeros((8, 128), jnp.float32)], axis=1),
            ],
            axis=0,
        )
        right_high, right_low = split(right)
        left_high, left_low = split(left)
        main = nt(jnp.concatenate([left_high, left_low], axis=0), right_high)
        total = main[:16] + main[16:] + nt(left_high, right_low)
        target = target_ref[q]
        row = target // (16 * BLOCKS)
        slot = used_ref[row]
        used_ref[row] = slot + 1
        place = pl.multiple_of(row * SHARE + slot * 8, 8)
        out_ref[pl.ds(place, 8), :] = jnp.where(first_half, total[:8], total[8:])
        block = (target % BLOCKS).astype(jnp.float32)
        out_ref[pl.ds(row * SHARE + SLOTS * 8 + slot, 1), :] = jnp.full((1, 128), block, jnp.float32)


def local_names(table, base):
    named = table.astype(jnp.int32)
    local = named - base
    return jnp.where((named >= 0) & (local >= 0) & (local < WINDOW), 8 * local, 8 * WINDOW)


def window_base():
    quad = lax.axis_index("scan") * lax.axis_size("quad") + lax.axis_index("quad")
    return (4 * quad - 2) * BLOCKS


def combine_kernel(parts_ref, near_ref, out_ref):
    sums = [jnp.zeros((8, 128), jnp.float32) for _ in range(BLOCKS)]
    for source in range(8):
        for slot in range(SLOTS):
            at = source * SHARE
            part = parts_ref[at + slot * 8 : at + slot * 8 + 8, :]
            name = jnp.broadcast_to(parts_ref[at + SLOTS * 8 + slot : at + SLOTS * 8 + slot + 1, :], (8, 128))
            for block in range(BLOCKS):
                sums[block] = sums[block] + jnp.where(name == float(block), part, 0.0)
    for block in range(BLOCKS):
        out_ref[block] = sums[block]
    out_ref[BLOCKS] = jnp.full((8, 128), -1.0, jnp.float32)
    out_ref[BLOCKS, :, 0:27] = near_ref[...].astype(jnp.float32)


def pack_kernel(own_ref, beside_ref, out_ref, longer_ref):
    longer_ref[2 * BLOCKS + 1] = own_ref[BLOCKS]
    for block in range(BLOCKS):
        out_ref[block] = own_ref[block]
        out_ref[BLOCKS + block] = beside_ref[block]
        longer_ref[block] = own_ref[block]
        longer_ref[BLOCKS + block] = beside_ref[block]
    tables = jnp.where(left_half(), own_ref[BLOCKS], pltpu.roll(beside_ref[BLOCKS], 64, 1))
    out_ref[2 * BLOCKS] = tables
    longer_ref[2 * BLOCKS] = tables


def doubled(tile, first_half):
    return jnp.where(first_half, tile, pltpu.roll(tile, 64, 1))


def rows_at(first):
    return pl.ds(pl.multiple_of(first, 8), 8)


def tile_at(block):
    return rows_at(8 * block)


def couple(lookup, blocks, wide_ref, rows_ref, table_ref):
    lane = lax.broadcasted_iota(jnp.int32, (8, 128), 1)
    sublane = lax.broadcasted_iota(jnp.int32, (8, 128), 0)
    first_half = lane < 64
    low_j = lane % 64 < 32
    low_k = lane % 8 < 4
    top = sublane == 0
    bottom = sublane == 7

    def tiles(block, shift):
        def plane(b, c):
            return wide_ref[rows_at(lookup(block, shift + 3 * (b + 1) + c + 1)), :]

        one = jnp.where(first_half, plane(0, 0), jnp.where(low_j, plane(1, 0), plane(-1, 0)))
        edges = jnp.where(low_k, plane(0, 1), plane(0, -1))
        corners = jnp.where(
            low_j,
            jnp.where(low_k, plane(1, 1), plane(1, -1)),
            jnp.where(low_k, plane(-1, 1), plane(-1, -1)),
        )
        return one, jnp.where(first_half, edges, corners)

    for block in range(blocks):
        before = tiles(block, 0)
        here = tiles(block, 9)
        after = tiles(block, 18)
        ends = [jnp.where(top, late, early) for early, late in zip(before, after)]
        rows = jnp.concatenate(
            [jnp.concatenate([here[half], ends[half]], axis=0) for half in range(2)], axis=1
        )
        high, low = split(rows)
        rows_ref[16 * block : 16 * block + 16, :] = high
        rows_ref[16 * (blocks + block) : 16 * (blocks + block) + 16, :] = low
    both = jnp.dot(rows_ref[0 : 32 * blocks, :], table_ref[...], preferred_element_type=jnp.float32)
    centre = jnp.where(first_half, 2.0 / 36.0, 4.0 / 36.0)
    side = jnp.where(first_half, -1.0 / 36.0, 1.0 / 36.0)
    result = []
    for block in range(blocks):
        at, other = 16 * block, 16 * (blocks + block)
        here = both[at : at + 8] + both[other : other + 8]
        ends = both[at + 8 : at + 16] + both[other + 8 : other + 16]
        before = pltpu.roll(jnp.where(bottom, ends, here), 1, 0)
        after = pltpu.roll(jnp.where(top, ends, here), 7, 0)
        value = centre * here + side * (before + after)
        result.append(value + pltpu.roll(value, 64, 1))
    return result


def total(lefts, rights, first_half):
    terms = [a * b for a, b in zip(lefts, rights)]
    while len(terms) > 1:
        terms = [a + b for a, b in zip(terms[::2], terms[1::2])]
    return jnp.sum(jnp.where(first_half, terms[0], 0.0), axis=(0, 1), keepdims=True)


def image_kernel(
    own_ref,
    one_ref,
    two_ref,
    three_ref,
    table_ref,
    first_ref,
    second_ref,
    sums_ref,
    wide_ref,
    next_ref,
    screen_ref,
    names_ref,
    short_ref,
    index_ref,
    rows_ref,
    done_ref,
):
    first_half = left_half()
    place = lax.axis_index("place")
    parts = []
    for step, ref in enumerate((own_ref, one_ref, two_ref, three_ref)):
        member = lax.bitwise_xor(place, step)
        parts.append((ref, (2 + member) * BLOCKS, lax.rem(member + 6, 8) * BLOCKS))
    for ref, inner, outer in parts:
        tile = ref[2 * BLOCKS]
        names_ref[pl.ds(pl.multiple_of(inner, 8), 8), :] = local_names(tile, window_base())
        names_ref[pl.ds(pl.multiple_of(outer, 8), 8), :] = local_names(pltpu.roll(tile, 64, 1), window_base())
    group = lax.broadcasted_iota(jnp.int32, (8, 128), 1) // 32
    for half, members in ((0, (1, 2, 3, 4)), (1, (5, 6))):
        tile = names_ref[8 * members[0] : 8 * members[0] + 8, :]
        for slot, member in enumerate(members[1:], 1):
            other = pltpu.roll(names_ref[8 * member : 8 * member + 8, :], 32 * slot, 1)
            tile = jnp.where(group == slot, other, tile)
        short_ref[8 * half : 8 * half + 8, :] = tile
    copy = pltpu.make_async_copy(short_ref, index_ref, done_ref)
    copy.start()
    for ref, inner, outer in parts:
        for block in range(2 * BLOCKS):
            at = inner + block if block < BLOCKS else outer + block - BLOCKS
            tile = ref[block]
            turned = pltpu.roll(tile, 64, 1)
            wide_ref[tile_at(at), :] = jnp.where(first_half, tile, turned)
            screen_ref[tile_at(at), :] = jnp.where(first_half, turned, tile)
    nothing = jnp.zeros((8, 128), jnp.float32)
    wide_ref[tile_at(WINDOW), :] = nothing
    next_ref[tile_at(WINDOW), :] = nothing
    copy.wait()

    def near(block, offset):
        device = block // BLOCKS
        return index_ref[device // 4 * BLOCKS + block % BLOCKS, device % 4 * 32 + offset]

    def inside(block, offset):
        return near(BLOCKS + block, offset)

    coupled = couple(near, 6 * BLOCKS, wide_ref, rows_ref, table_ref)
    for block in range(6 * BLOCKS):
        at = BLOCKS + block
        next_ref[tile_at(at), :] = screen_ref[tile_at(at), :] * wide_ref[tile_at(at), :] + coupled[block]
    start = [wide_ref[tile_at(2 * BLOCKS + block), :] for block in range(4 * BLOCKS)]
    first = [next_ref[tile_at(2 * BLOCKS + block), :] for block in range(4 * BLOCKS)]
    coupled = couple(inside, 4 * BLOCKS, next_ref, rows_ref, table_ref)
    second = []
    for block in range(4 * BLOCKS):
        image = screen_ref[tile_at(2 * BLOCKS + block), :] * first[block] + coupled[block]
        second.append(image)
        wide_ref[tile_at(block), :] = image
    for block in range(BLOCKS):
        first_ref[block] = next_ref[tile_at((2 + place) * BLOCKS + block), :]
        second_ref[block] = wide_ref[tile_at(place * BLOCKS + block), :]
    lane = lax.broadcasted_iota(jnp.int32, (1, 128), 1)
    line = jnp.zeros((1, 128), jnp.float32)
    pairs = ((start, start), (start, first), (first, first), (start, second), (first, second))
    for slot, (a, b) in enumerate(pairs):
        line = jnp.where(lane == slot, total(a, b, first_half), line)
    sums_ref[...] = jnp.broadcast_to(line, (32, 128))


def last_kernel(sums_ref, fields_ref, first_ref, second_ref, solution_ref, residual_ref, left_ref, right_ref):
    first_half = left_half()
    sums = jnp.sum(sums_ref[...], axis=0, keepdims=True)
    lane = lax.broadcasted_iota(jnp.int32, (1, 128), 1)

    def pick(place):
        return jnp.sum(jnp.where(lane == place, sums, 0.0), axis=1, keepdims=True)

    s00, s01, s11, s02, s12 = (pick(place) for place in range(5))
    alpha0 = s00 / s01
    norm1 = s00 - 2.0 * alpha0 * s01 + alpha0 * alpha0 * s11
    beta = norm1 / s00
    grow = 1.0 + beta
    curve = grow * grow * s01 - grow * alpha0 * (s02 + s11) + alpha0 * alpha0 * s12
    alpha1 = norm1 / curve
    for block in range(BLOCKS):
        start = doubled(fields_ref[block], first_half)
        first = first_ref[block]
        left = start - alpha0 * first
        direction = left + beta * start
        image = grow * first - alpha0 * second_ref[block]
        left_ref[block] = alpha0 * start + alpha1 * direction
        right_ref[block] = left - alpha1 * image
    for pair in range(4):
        lanes = slice(128 * pair, 128 * pair + 128)
        solution_ref[:, lanes] = jnp.where(first_half, left_ref[:, 2 * pair, :], left_ref[:, 2 * pair + 1, :])
        residual_ref[:, lanes] = jnp.where(first_half, right_ref[:, 2 * pair, :], right_ref[:, 2 * pair + 1, :])


def vmem(count):
    return [pl.BlockSpec(memory_space=pltpu.VMEM)] * count


def smem(count):
    return [pl.BlockSpec(memory_space=pltpu.SMEM)] * count


def shape(*dims):
    return pltpu.VMEM(dims, jnp.float32)


def resident(values):
    return pltpu.with_memory_space_constraint(values, pltpu.VMEM)


def per_device(positions, normals, weights, point_target, neighbours):
    table = resident(jnp.asarray(plane_table(), jnp.bfloat16))
    parts = pl.pallas_call(
        splat_kernel,
        out_shape=shape(8 * SHARE, 128),
        in_specs=smem(1) + vmem(3),
        out_specs=vmem(1)[0],
        scratch_shapes=[pltpu.SMEM((8,), jnp.int32)],
        name="splat",
    )(point_target, positions.transpose(1, 0, 2), normals.transpose(1, 0, 2), weights)
    parts = resident(lax.all_to_all(parts, "scan", 0, 0, tiled=True))
    fields = resident(
        pl.pallas_call(
            combine_kernel,
            out_shape=shape(BLOCKS + 1, 8, 128),
            in_specs=vmem(2),
            out_specs=vmem(1)[0],
            name="combine",
        )(parts, resident(neighbours))
    )
    count = lax.axis_size("scan") * lax.axis_size("quad") * 4
    beside = resident(lax.ppermute(fields, ALL, [(i, (i - 4 if i % 4 < 2 else i + 4) % count) for i in range(count)]))
    packed, longer = pl.pallas_call(
        pack_kernel,
        out_shape=(shape(2 * BLOCKS + 1, 8, 128), shape(2 * BLOCKS + 2, 8, 128)),
        in_specs=vmem(2),
        out_specs=tuple(vmem(2)),
        name="pack",
    )(fields, beside)
    others = [
        resident(lax.ppermute(longer if step == 2 else packed, "place", [(i, i ^ step) for i in range(4)]))
        for step in (1, 2, 3)
    ]
    first, second, sums = pl.pallas_call(
        image_kernel,
        out_shape=(shape(BLOCKS, 8, 128), shape(BLOCKS, 8, 128), shape(32, 128)),
        in_specs=vmem(5),
        out_specs=tuple(vmem(3)),
        scratch_shapes=[
            pltpu.VMEM((8 * WINDOW + 8, 128), jnp.float32),
            pltpu.VMEM((8 * WINDOW + 8, 128), jnp.float32),
            pltpu.VMEM((8 * WINDOW, 128), jnp.float32),
            pltpu.VMEM((WINDOW, 128), jnp.int32),
            pltpu.VMEM((2 * BLOCKS, 128), jnp.int32),
            pltpu.SMEM((2 * BLOCKS, 128), jnp.int32),
            pltpu.VMEM((6 * BLOCKS * 32, 256), jnp.bfloat16),
            pltpu.SemaphoreType.DMA,
        ],
        name="images",
    )(resident(packed), *others, table)
    sums = resident(lax.all_to_all(sums, ("scan", "quad"), 0, 0, tiled=True))
    return pl.pallas_call(
        last_kernel,
        out_shape=(jax.ShapeDtypeStruct((BLOCKS, 512), jnp.float32),) * 2,
        in_specs=vmem(4),
        out_specs=tuple(vmem(2)),
        scratch_shapes=[pltpu.VMEM((BLOCKS, 8, 128), jnp.float32)] * 2,
        name="last",
    )(sums, fields, resident(first), resident(second))


def solution(mesh):
    scan, morton = mesh.devices.shape
    grouped = Mesh(mesh.devices.reshape(scan, morton // 4, 4), ALL)
    placed = (P(ALL, None, None), P(ALL, None, None), P(ALL, None), P(ALL), P(ALL, None))
    return jax.shard_map(
        per_device,
        mesh=grouped,
        in_specs=placed,
        out_specs=(P(ALL, None), P(ALL, None)),
        check_vma=False,
    )
```

```python
import jax
import jax.numpy as jnp
import numpy as np
from jax import lax
from jax.experimental import pallas as pl
from jax.experimental.pallas import tpu as pltpu
from jax.sharding import Mesh
from jax.sharding import PartitionSpec as P

SCREEN = 16.0
BLOCKS = 8
SLOTS = 4
SHARE = SLOTS * 8 + 1
ROOM = SLOTS * 8 + 8
ALL = ("scan", "quad", "place")
WINDOW = 8 * BLOCKS


def plane_table():
    mass = {-1: 1.0, 0: 4.0, 1: 1.0}
    stiff = {-1: -1.0, 0: 2.0, 1: -1.0}
    side = {0: 1, 7: -1}
    table = np.zeros((256, 128), np.float32)
    for group in range(4):
        for row in range(64):
            b = side.get(row // 8) if group in (1, 3) else 0
            c = side.get(row % 8) if group in (2, 3) else 0
            if b is None or c is None:
                continue
            for col in range(64):
                dj = 8 * b + row // 8 - col // 8
                dk = 8 * c + row % 8 - col % 8
                if abs(dj) <= 1 and abs(dk) <= 1:
                    table[64 * group + row, col] = mass[dj] * mass[dk]
                    table[64 * group + row, 64 + col] = stiff[dj] * mass[dk] + mass[dj] * stiff[dk]
    return table


def split(values):
    high = values.astype(jnp.bfloat16)
    low = (values - high.astype(jnp.float32)).astype(jnp.bfloat16)
    return high, low


def nt(left, right):
    return lax.dot_general(left, right, (((1,), (1,)), ((), ())), preferred_element_type=jnp.float32)


def left_half():
    return lax.broadcasted_iota(jnp.int32, (8, 128), 1) < 64


def splat_kernel(target_ref, spots_ref, norms_ref, weights_ref, out_ref, used_ref, work_ref):
    node = lax.broadcasted_iota(jnp.int32, (8, 128), 0).astype(jnp.float32)
    first_half = left_half()
    nothing = jnp.zeros((64, 128), jnp.float32)
    for row in range(8):
        used_ref[row] = 0
        work_ref[row * ROOM + SLOTS * 8 : (row + 1) * ROOM, :] = jnp.full((8, 128), -1.0, jnp.float32)
    for q in range(16):
        hats, slopes = [], []
        for dim in range(3):
            diff = spots_ref[dim, q : q + 1, :] - node
            dist = jnp.abs(diff)
            hats.append(jnp.maximum(0.0, 1.0 - dist))
            way = jnp.where(diff > 0.0, -1.0, jnp.where(diff < 0.0, 1.0, 0.0))
            slopes.append(jnp.where(dist < 1.0, way, 0.0))
        weight = weights_ref[q : q + 1, :]
        one = weight * norms_ref[0, q : q + 1, :] * slopes[0]
        two = weight * hats[0]
        three = SCREEN * two * hats[0]
        slope1 = norms_ref[1, q : q + 1, :] * slopes[1]
        slope2 = norms_ref[2, q : q + 1, :] * slopes[2]
        square1 = hats[1] * hats[1]
        square2 = hats[2] * hats[2]
        first = jnp.concatenate([hats[1][j : j + 1] * hats[2] for j in range(8)], axis=0)
        second = jnp.concatenate(
            [slope1[j : j + 1] * hats[2] + hats[1][j : j + 1] * slope2 for j in range(8)], axis=0
        )
        outer = jnp.concatenate([square1[j : j + 1] * square2 for j in range(8)], axis=0)
        right = jnp.concatenate(
            [jnp.concatenate([first, second], axis=1), jnp.concatenate([outer, nothing], axis=1)], axis=0
        )
        left = jnp.concatenate(
            [
                jnp.concatenate([one, two], axis=1),
                jnp.concatenate([three, jnp.zeros((8, 128), jnp.float32)], axis=1),
            ],
            axis=0,
        )
        right_high, right_low = split(right)
        left_high, left_low = split(left)
        main = nt(jnp.concatenate([left_high, left_low], axis=0), right_high)
        total = main[:16] + main[16:] + nt(left_high, right_low)
        target = target_ref[q]
        row = target // (16 * BLOCKS)
        slot = used_ref[row]
        used_ref[row] = slot + 1
        place = pl.multiple_of(row * ROOM + slot * 8, 8)
        work_ref[pl.ds(place, 8), :] = jnp.where(first_half, total[:8], total[8:])
        block = (target % BLOCKS).astype(jnp.float32)
        work_ref[pl.ds(row * ROOM + SLOTS * 8 + slot, 1), :] = jnp.full((1, 128), block, jnp.float32)
    group = lax.broadcasted_iota(jnp.int32, (1, 128), 1) // 32
    for row in range(8):
        at = row * ROOM + SLOTS * 8
        out_ref[row * SHARE : row * SHARE + SLOTS * 8, :] = work_ref[row * ROOM : at, :]
        names = work_ref[at : at + 1, :]
        for slot in range(1, SLOTS):
            names = jnp.where(group == slot, work_ref[at + slot : at + slot + 1, :], names)
        out_ref[row * SHARE + SLOTS * 8 : (row + 1) * SHARE, :] = names


def local_names(table, base):
    named = table.astype(jnp.int32)
    local = named - base
    return jnp.where((named >= 0) & (local >= 0) & (local < WINDOW), 8 * local, 8 * WINDOW)


def window_base():
    quad = lax.axis_index("scan") * lax.axis_size("quad") + lax.axis_index("quad")
    return (4 * quad - 2) * BLOCKS


def combine_kernel(parts_ref, near_ref, out_ref):
    sums = [jnp.zeros((8, 128), jnp.float32) for _ in range(BLOCKS)]
    for source in range(8):
        at = source * SHARE
        names = parts_ref[at + SLOTS * 8 : at + SHARE, :]
        for slot in range(SLOTS):
            part = parts_ref[at + slot * 8 : at + slot * 8 + 8, :]
            name = jnp.broadcast_to(names[:, 32 * slot : 32 * slot + 1], (8, 128))
            for block in range(BLOCKS):
                sums[block] = sums[block] + jnp.where(name == float(block), part, 0.0)
    for block in range(BLOCKS):
        out_ref[block] = sums[block]
    out_ref[BLOCKS] = jnp.full((8, 128), -1.0, jnp.float32)
    out_ref[BLOCKS, :, 0:27] = near_ref[...].astype(jnp.float32)


def pack_kernel(own_ref, beside_ref, out_ref, longer_ref):
    longer_ref[2 * BLOCKS + 1] = own_ref[BLOCKS]
    for block in range(BLOCKS):
        out_ref[block] = own_ref[block]
        out_ref[BLOCKS + block] = beside_ref[block]
        longer_ref[block] = own_ref[block]
        longer_ref[BLOCKS + block] = beside_ref[block]
    tables = jnp.where(left_half(), own_ref[BLOCKS], pltpu.roll(beside_ref[BLOCKS], 64, 1))
    out_ref[2 * BLOCKS] = tables
    longer_ref[2 * BLOCKS] = tables


def doubled(tile, first_half):
    return jnp.where(first_half, tile, pltpu.roll(tile, 64, 1))


def rows_at(first):
    return pl.ds(pl.multiple_of(first, 8), 8)


def tile_at(block):
    return rows_at(8 * block)


def couple(lookup, blocks, wide_ref, rows_ref, table_ref):
    lane = lax.broadcasted_iota(jnp.int32, (8, 128), 1)
    sublane = lax.broadcasted_iota(jnp.int32, (8, 128), 0)
    first_half = lane < 64
    low_j = lane % 64 < 32
    low_k = lane % 8 < 4
    top = sublane == 0
    bottom = sublane == 7

    def tiles(block, shift):
        def plane(b, c):
            return wide_ref[rows_at(lookup(block, shift + 3 * (b + 1) + c + 1)), :]

        one = jnp.where(first_half, plane(0, 0), jnp.where(low_j, plane(1, 0), plane(-1, 0)))
        edges = jnp.where(low_k, plane(0, 1), plane(0, -1))
        corners = jnp.where(
            low_j,
            jnp.where(low_k, plane(1, 1), plane(1, -1)),
            jnp.where(low_k, plane(-1, 1), plane(-1, -1)),
        )
        return one, jnp.where(first_half, edges, corners)

    for block in range(blocks):
        before = tiles(block, 0)
        here = tiles(block, 9)
        after = tiles(block, 18)
        ends = [jnp.where(top, late, early) for early, late in zip(before, after)]
        rows = jnp.concatenate(
            [jnp.concatenate([here[half], ends[half]], axis=0) for half in range(2)], axis=1
        )
        high, low = split(rows)
        rows_ref[16 * block : 16 * block + 16, 0:256] = high
        rows_ref[16 * block : 16 * block + 16, 256:512] = low
    sums = jnp.dot(rows_ref[0 : 16 * blocks, :], table_ref[...], preferred_element_type=jnp.float32)
    centre = jnp.where(first_half, 2.0 / 36.0, 4.0 / 36.0)
    side = jnp.where(first_half, -1.0 / 36.0, 1.0 / 36.0)
    result = []
    for block in range(blocks):
        here = sums[16 * block : 16 * block + 8]
        ends = sums[16 * block + 8 : 16 * block + 16]
        before = pltpu.roll(jnp.where(bottom, ends, here), 1, 0)
        after = pltpu.roll(jnp.where(top, ends, here), 7, 0)
        value = centre * here + side * (before + after)
        result.append(value + pltpu.roll(value, 64, 1))
    return result


def total(lefts, rights, first_half):
    terms = [a * b for a, b in zip(lefts, rights)]
    while len(terms) > 1:
        terms = [a + b for a, b in zip(terms[::2], terms[1::2])]
    return jnp.sum(jnp.where(first_half, terms[0], 0.0), axis=(0, 1), keepdims=True)


def image_kernel(
    own_ref,
    one_ref,
    two_ref,
    three_ref,
    table_ref,
    first_ref,
    second_ref,
    sums_ref,
    wide_ref,
    next_ref,
    screen_ref,
    names_ref,
    short_ref,
    index_ref,
    rows_ref,
    done_ref,
):
    first_half = left_half()
    place = lax.axis_index("place")
    parts = []
    for step, ref in enumerate((own_ref, one_ref, two_ref, three_ref)):
        member = lax.bitwise_xor(place, step)
        parts.append((ref, (2 + member) * BLOCKS, lax.rem(member + 6, 8) * BLOCKS))
    for ref, inner, outer in parts:
        tile = ref[2 * BLOCKS]
        names_ref[pl.ds(pl.multiple_of(inner, 8), 8), :] = local_names(tile, window_base())
        names_ref[pl.ds(pl.multiple_of(outer, 8), 8), :] = local_names(pltpu.roll(tile, 64, 1), window_base())
    group = lax.broadcasted_iota(jnp.int32, (8, 128), 1) // 32
    for half, members in ((0, (1, 2, 3, 4)), (1, (5, 6))):
        tile = names_ref[8 * members[0] : 8 * members[0] + 8, :]
        for slot, member in enumerate(members[1:], 1):
            other = pltpu.roll(names_ref[8 * member : 8 * member + 8, :], 32 * slot, 1)
            tile = jnp.where(group == slot, other, tile)
        short_ref[8 * half : 8 * half + 8, :] = tile
    copy = pltpu.make_async_copy(short_ref, index_ref, done_ref)
    copy.start()
    for ref, inner, outer in parts:
        for block in range(2 * BLOCKS):
            at = inner + block if block < BLOCKS else outer + block - BLOCKS
            tile = ref[block]
            turned = pltpu.roll(tile, 64, 1)
            wide_ref[tile_at(at), :] = jnp.where(first_half, tile, turned)
            screen_ref[tile_at(at), :] = jnp.where(first_half, turned, tile)
    nothing = jnp.zeros((8, 128), jnp.float32)
    wide_ref[tile_at(WINDOW), :] = nothing
    next_ref[tile_at(WINDOW), :] = nothing
    copy.wait()

    def near(block, offset):
        device = block // BLOCKS
        return index_ref[device // 4 * BLOCKS + block % BLOCKS, device % 4 * 32 + offset]

    def inside(block, offset):
        return near(BLOCKS + block, offset)

    coupled = couple(near, 6 * BLOCKS, wide_ref, rows_ref, table_ref)
    for block in range(6 * BLOCKS):
        at = BLOCKS + block
        next_ref[tile_at(at), :] = screen_ref[tile_at(at), :] * wide_ref[tile_at(at), :] + coupled[block]
    start = [wide_ref[tile_at(2 * BLOCKS + block), :] for block in range(4 * BLOCKS)]
    first = [next_ref[tile_at(2 * BLOCKS + block), :] for block in range(4 * BLOCKS)]
    coupled = couple(inside, 4 * BLOCKS, next_ref, rows_ref, table_ref)
    second = []
    for block in range(4 * BLOCKS):
        image = screen_ref[tile_at(2 * BLOCKS + block), :] * first[block] + coupled[block]
        second.append(image)
        wide_ref[tile_at(block), :] = image
    for block in range(BLOCKS):
        first_ref[block] = next_ref[tile_at((2 + place) * BLOCKS + block), :]
        second_ref[block] = wide_ref[tile_at(place * BLOCKS + block), :]
    lane = lax.broadcasted_iota(jnp.int32, (1, 128), 1)
    line = jnp.zeros((1, 128), jnp.float32)
    pairs = ((start, start), (start, first), (first, first), (start, second), (first, second))
    for slot, (a, b) in enumerate(pairs):
        line = jnp.where(lane == slot, total(a, b, first_half), line)
    sums_ref[...] = jnp.broadcast_to(line, (32, 128))


def last_kernel(sums_ref, fields_ref, first_ref, second_ref, solution_ref, residual_ref, left_ref, right_ref):
    first_half = left_half()
    sums = jnp.sum(sums_ref[...], axis=0, keepdims=True)
    lane = lax.broadcasted_iota(jnp.int32, (1, 128), 1)

    def pick(place):
        return jnp.sum(jnp.where(lane == place, sums, 0.0), axis=1, keepdims=True)

    s00, s01, s11, s02, s12 = (pick(place) for place in range(5))
    alpha0 = s00 / s01
    norm1 = s00 - 2.0 * alpha0 * s01 + alpha0 * alpha0 * s11
    beta = norm1 / s00
    grow = 1.0 + beta
    curve = grow * grow * s01 - grow * alpha0 * (s02 + s11) + alpha0 * alpha0 * s12
    alpha1 = norm1 / curve
    for block in range(BLOCKS):
        start = doubled(fields_ref[block], first_half)
        first = first_ref[block]
        left = start - alpha0 * first
        direction = left + beta * start
        image = grow * first - alpha0 * second_ref[block]
        left_ref[block] = alpha0 * start + alpha1 * direction
        right_ref[block] = left - alpha1 * image
    for pair in range(4):
        lanes = slice(128 * pair, 128 * pair + 128)
        solution_ref[:, lanes] = jnp.where(first_half, left_ref[:, 2 * pair, :], left_ref[:, 2 * pair + 1, :])
        residual_ref[:, lanes] = jnp.where(first_half, right_ref[:, 2 * pair, :], right_ref[:, 2 * pair + 1, :])


def vmem(count):
    return [pl.BlockSpec(memory_space=pltpu.VMEM)] * count


def smem(count):
    return [pl.BlockSpec(memory_space=pltpu.SMEM)] * count


def shape(*dims):
    return pltpu.VMEM(dims, jnp.float32)


def resident(values):
    return pltpu.with_memory_space_constraint(values, pltpu.VMEM)


def per_device(positions, normals, weights, point_target, neighbours):
    table = resident(jnp.asarray(np.concatenate([plane_table()] * 2), jnp.bfloat16))
    parts = pl.pallas_call(
        splat_kernel,
        out_shape=shape(8 * SHARE, 128),
        in_specs=smem(1) + vmem(3),
        out_specs=vmem(1)[0],
        scratch_shapes=[pltpu.SMEM((8,), jnp.int32), pltpu.VMEM((8 * ROOM, 128), jnp.float32)],
        name="splat",
    )(point_target, positions.transpose(1, 0, 2), normals.transpose(1, 0, 2), weights)
    parts = lax.all_to_all(parts.reshape(8, 1, SHARE * 128), "scan", 0, 0, tiled=True)
    parts = resident(parts.reshape(8 * SHARE, 128))
    fields = resident(
        pl.pallas_call(
            combine_kernel,
            out_shape=shape(BLOCKS + 1, 8, 128),
            in_specs=vmem(2),
            out_specs=vmem(1)[0],
            name="combine",
        )(parts, resident(neighbours))
    )
    count = lax.axis_size("scan") * lax.axis_size("quad") * 4
    beside = resident(lax.ppermute(fields, ALL, [(i, (i - 4 if i % 4 < 2 else i + 4) % count) for i in range(count)]))
    packed, longer = pl.pallas_call(
        pack_kernel,
        out_shape=(shape(2 * BLOCKS + 1, 8, 128), shape(2 * BLOCKS + 2, 8, 128)),
        in_specs=vmem(2),
        out_specs=tuple(vmem(2)),
        name="pack",
    )(fields, beside)
    others = [
        resident(lax.ppermute(longer if step == 2 else packed, "place", [(i, i ^ step) for i in range(4)]))
        for step in (1, 2, 3)
    ]
    first, second, sums = pl.pallas_call(
        image_kernel,
        out_shape=(shape(BLOCKS, 8, 128), shape(BLOCKS, 8, 128), shape(32, 128)),
        in_specs=vmem(5),
        out_specs=tuple(vmem(3)),
        scratch_shapes=[
            pltpu.VMEM((8 * WINDOW + 8, 128), jnp.float32),
            pltpu.VMEM((8 * WINDOW + 8, 128), jnp.float32),
            pltpu.VMEM((8 * WINDOW, 128), jnp.float32),
            pltpu.VMEM((WINDOW, 128), jnp.int32),
            pltpu.VMEM((2 * BLOCKS, 128), jnp.int32),
            pltpu.SMEM((2 * BLOCKS, 128), jnp.int32),
            pltpu.VMEM((6 * BLOCKS * 16, 512), jnp.bfloat16),
            pltpu.SemaphoreType.DMA,
        ],
        name="images",
    )(resident(packed), *others, table)
    sums = resident(lax.all_to_all(sums, ("scan", "quad"), 0, 0, tiled=True))
    return pl.pallas_call(
        last_kernel,
        out_shape=(jax.ShapeDtypeStruct((BLOCKS, 512), jnp.float32),) * 2,
        in_specs=vmem(4),
        out_specs=tuple(vmem(2)),
        scratch_shapes=[pltpu.VMEM((BLOCKS, 8, 128), jnp.float32)] * 2,
        name="last",
    )(sums, fields, resident(first), resident(second))


def solution(mesh):
    scan, morton = mesh.devices.shape
    grouped = Mesh(mesh.devices.reshape(scan, morton // 4, 4), ALL)
    placed = (P(ALL, None, None), P(ALL, None, None), P(ALL, None), P(ALL), P(ALL, None))
    return jax.shard_map(
        per_device,
        mesh=grouped,
        in_specs=placed,
        out_specs=(P(ALL, None), P(ALL, None)),
        check_vma=False,
    )
```

```python
import jax
import jax.numpy as jnp
import numpy as np
from jax import lax
from jax.experimental import pallas as pl
from jax.experimental.pallas import tpu as pltpu
from jax.sharding import Mesh
from jax.sharding import PartitionSpec as P

SCREEN = 16.0
BLOCKS = 8
SLOTS = 4
SHARE = SLOTS * 9
ROOM = SLOTS * 8 + 8
ALL = ("scan", "quad", "place")
WINDOW = 8 * BLOCKS


def plane_table():
    mass = {-1: 1.0, 0: 4.0, 1: 1.0}
    stiff = {-1: -1.0, 0: 2.0, 1: -1.0}
    side = {0: 1, 7: -1}
    table = np.zeros((256, 128), np.float32)
    for group in range(4):
        for row in range(64):
            b = side.get(row // 8) if group in (1, 3) else 0
            c = side.get(row % 8) if group in (2, 3) else 0
            if b is None or c is None:
                continue
            for col in range(64):
                dj = 8 * b + row // 8 - col // 8
                dk = 8 * c + row % 8 - col % 8
                if abs(dj) <= 1 and abs(dk) <= 1:
                    table[64 * group + row, col] = mass[dj] * mass[dk]
                    table[64 * group + row, 64 + col] = stiff[dj] * mass[dk] + mass[dj] * stiff[dk]
    return table


def split(values):
    high = values.astype(jnp.bfloat16)
    low = (values - high.astype(jnp.float32)).astype(jnp.bfloat16)
    return high, low


def nt(left, right):
    return lax.dot_general(left, right, (((1,), (1,)), ((), ())), preferred_element_type=jnp.float32)


def left_half():
    return lax.broadcasted_iota(jnp.int32, (8, 128), 1) < 64


def splat_kernel(target_ref, spots_ref, norms_ref, weights_ref, out_ref, used_ref, work_ref):
    node = lax.broadcasted_iota(jnp.int32, (8, 128), 0).astype(jnp.float32)
    first_half = left_half()
    nothing = jnp.zeros((64, 128), jnp.float32)
    for row in range(8):
        used_ref[row] = 0
        work_ref[row * ROOM + SLOTS * 8 : (row + 1) * ROOM, :] = jnp.full((8, 128), -1.0, jnp.float32)
    for q in range(16):
        hats, slopes = [], []
        for dim in range(3):
            diff = spots_ref[dim, q : q + 1, :] - node
            dist = jnp.abs(diff)
            hats.append(jnp.maximum(0.0, 1.0 - dist))
            way = jnp.where(diff > 0.0, -1.0, jnp.where(diff < 0.0, 1.0, 0.0))
            slopes.append(jnp.where(dist < 1.0, way, 0.0))
        weight = weights_ref[q : q + 1, :]
        one = weight * norms_ref[0, q : q + 1, :] * slopes[0]
        two = weight * hats[0]
        three = SCREEN * two * hats[0]
        slope1 = norms_ref[1, q : q + 1, :] * slopes[1]
        slope2 = norms_ref[2, q : q + 1, :] * slopes[2]
        square1 = hats[1] * hats[1]
        square2 = hats[2] * hats[2]
        first = jnp.concatenate([hats[1][j : j + 1] * hats[2] for j in range(8)], axis=0)
        second = jnp.concatenate(
            [slope1[j : j + 1] * hats[2] + hats[1][j : j + 1] * slope2 for j in range(8)], axis=0
        )
        outer = jnp.concatenate([square1[j : j + 1] * square2 for j in range(8)], axis=0)
        right = jnp.concatenate(
            [jnp.concatenate([first, second], axis=1), jnp.concatenate([outer, nothing], axis=1)], axis=0
        )
        left = jnp.concatenate(
            [
                jnp.concatenate([one, two], axis=1),
                jnp.concatenate([three, jnp.zeros((8, 128), jnp.float32)], axis=1),
            ],
            axis=0,
        )
        right_high, right_low = split(right)
        left_high, left_low = split(left)
        main = nt(jnp.concatenate([left_high, left_low], axis=0), right_high)
        total = main[:16] + main[16:] + nt(left_high, right_low)
        target = target_ref[q]
        row = target // (16 * BLOCKS)
        slot = used_ref[row]
        used_ref[row] = slot + 1
        place = pl.multiple_of(row * ROOM + slot * 8, 8)
        work_ref[pl.ds(place, 8), :] = jnp.where(first_half, total[:8], total[8:])
        block = (target % BLOCKS).astype(jnp.float32)
        work_ref[pl.ds(row * ROOM + SLOTS * 8 + slot, 1), :] = jnp.full((1, 128), block, jnp.float32)
    for row in range(8):
        out_ref[row * SHARE : (row + 1) * SHARE, :] = work_ref[row * ROOM : row * ROOM + SHARE, :]


def local_names(table, base):
    named = table.astype(jnp.int32)
    local = named - base
    return jnp.where((named >= 0) & (local >= 0) & (local < WINDOW), 8 * local, 8 * WINDOW)


def window_base():
    quad = lax.axis_index("scan") * lax.axis_size("quad") + lax.axis_index("quad")
    return (4 * quad - 2) * BLOCKS


def combine_kernel(parts_ref, near_ref, out_ref):
    sums = [jnp.zeros((8, 128), jnp.float32) for _ in range(BLOCKS)]
    for source in range(8):
        at = source * SHARE
        names = parts_ref[at + SLOTS * 8 : at + SHARE, :]
        for slot in range(SLOTS):
            part = parts_ref[at + slot * 8 : at + slot * 8 + 8, :]
            name = jnp.broadcast_to(names[slot : slot + 1, :], (8, 128))
            for block in range(BLOCKS):
                sums[block] = sums[block] + jnp.where(name == float(block), part, 0.0)
    for block in range(BLOCKS):
        out_ref[block] = sums[block]
    out_ref[BLOCKS] = jnp.full((8, 128), -1.0, jnp.float32)
    out_ref[BLOCKS, :, 0:27] = near_ref[...].astype(jnp.float32)


def pack_kernel(own_ref, beside_ref, out_ref, longer_ref):
    longer_ref[2 * BLOCKS + 1] = own_ref[BLOCKS]
    for block in range(BLOCKS):
        out_ref[block] = own_ref[block]
        out_ref[BLOCKS + block] = beside_ref[block]
        longer_ref[block] = own_ref[block]
        longer_ref[BLOCKS + block] = beside_ref[block]
    tables = jnp.where(left_half(), own_ref[BLOCKS], pltpu.roll(beside_ref[BLOCKS], 64, 1))
    out_ref[2 * BLOCKS] = tables
    longer_ref[2 * BLOCKS] = tables


def doubled(tile, first_half):
    return jnp.where(first_half, tile, pltpu.roll(tile, 64, 1))


def rows_at(first):
    return pl.ds(pl.multiple_of(first, 8), 8)


def tile_at(block):
    return rows_at(8 * block)


def couple(lookup, blocks, wide_ref, rows_ref, table_ref):
    lane = lax.broadcasted_iota(jnp.int32, (8, 128), 1)
    sublane = lax.broadcasted_iota(jnp.int32, (8, 128), 0)
    first_half = lane < 64
    low_j = lane % 64 < 32
    low_k = lane % 8 < 4
    top = sublane == 0
    bottom = sublane == 7

    def tiles(block, shift):
        def plane(b, c):
            return wide_ref[rows_at(lookup(block, shift + 3 * (b + 1) + c + 1)), :]

        one = jnp.where(first_half, plane(0, 0), jnp.where(low_j, plane(1, 0), plane(-1, 0)))
        edges = jnp.where(low_k, plane(0, 1), plane(0, -1))
        corners = jnp.where(
            low_j,
            jnp.where(low_k, plane(1, 1), plane(1, -1)),
            jnp.where(low_k, plane(-1, 1), plane(-1, -1)),
        )
        return one, jnp.where(first_half, edges, corners)

    for block in range(blocks):
        before = tiles(block, 0)
        here = tiles(block, 9)
        after = tiles(block, 18)
        ends = [jnp.where(top, late, early) for early, late in zip(before, after)]
        rows = jnp.concatenate(
            [jnp.concatenate([here[half], ends[half]], axis=0) for half in range(2)], axis=1
        )
        high, low = split(rows)
        rows_ref[16 * block : 16 * block + 16, 0:256] = high
        rows_ref[16 * block : 16 * block + 16, 256:512] = low
    sums = jnp.dot(rows_ref[0 : 16 * blocks, :], table_ref[...], preferred_element_type=jnp.float32)
    centre = jnp.where(first_half, 2.0 / 36.0, 4.0 / 36.0)
    side = jnp.where(first_half, -1.0 / 36.0, 1.0 / 36.0)
    result = []
    for block in range(blocks):
        here = sums[16 * block : 16 * block + 8]
        ends = sums[16 * block + 8 : 16 * block + 16]
        before = pltpu.roll(jnp.where(bottom, ends, here), 1, 0)
        after = pltpu.roll(jnp.where(top, ends, here), 7, 0)
        value = centre * here + side * (before + after)
        result.append(value + pltpu.roll(value, 64, 1))
    return result


def total(lefts, rights, first_half):
    terms = [a * b for a, b in zip(lefts, rights)]
    while len(terms) > 1:
        terms = [a + b for a, b in zip(terms[::2], terms[1::2])]
    return jnp.sum(jnp.where(first_half, terms[0], 0.0), axis=(0, 1), keepdims=True)


def image_kernel(
    own_ref,
    one_ref,
    two_ref,
    three_ref,
    table_ref,
    first_ref,
    second_ref,
    sums_ref,
    wide_ref,
    next_ref,
    screen_ref,
    names_ref,
    short_ref,
    index_ref,
    rows_ref,
    done_ref,
):
    first_half = left_half()
    place = lax.axis_index("place")
    parts = []
    for step, ref in enumerate((own_ref, one_ref, two_ref, three_ref)):
        member = lax.bitwise_xor(place, step)
        parts.append((ref, (2 + member) * BLOCKS, lax.rem(member + 6, 8) * BLOCKS))
    for ref, inner, outer in parts:
        tile = ref[2 * BLOCKS]
        names_ref[pl.ds(pl.multiple_of(inner, 8), 8), :] = local_names(tile, window_base())
        names_ref[pl.ds(pl.multiple_of(outer, 8), 8), :] = local_names(pltpu.roll(tile, 64, 1), window_base())
    group = lax.broadcasted_iota(jnp.int32, (8, 128), 1) // 32
    for half, members in ((0, (1, 2, 3, 4)), (1, (5, 6))):
        tile = names_ref[8 * members[0] : 8 * members[0] + 8, :]
        for slot, member in enumerate(members[1:], 1):
            other = pltpu.roll(names_ref[8 * member : 8 * member + 8, :], 32 * slot, 1)
            tile = jnp.where(group == slot, other, tile)
        short_ref[8 * half : 8 * half + 8, :] = tile
    copy = pltpu.make_async_copy(short_ref, index_ref, done_ref)
    copy.start()
    for ref, inner, outer in parts:
        for block in range(2 * BLOCKS):
            at = inner + block if block < BLOCKS else outer + block - BLOCKS
            tile = ref[block]
            turned = pltpu.roll(tile, 64, 1)
            wide_ref[tile_at(at), :] = jnp.where(first_half, tile, turned)
            screen_ref[tile_at(at), :] = jnp.where(first_half, turned, tile)
    nothing = jnp.zeros((8, 128), jnp.float32)
    wide_ref[tile_at(WINDOW), :] = nothing
    next_ref[tile_at(WINDOW), :] = nothing
    copy.wait()

    def near(block, offset):
        device = block // BLOCKS
        return index_ref[device // 4 * BLOCKS + block % BLOCKS, device % 4 * 32 + offset]

    def inside(block, offset):
        return near(BLOCKS + block, offset)

    coupled = couple(near, 6 * BLOCKS, wide_ref, rows_ref, table_ref)
    for block in range(6 * BLOCKS):
        at = BLOCKS + block
        next_ref[tile_at(at), :] = screen_ref[tile_at(at), :] * wide_ref[tile_at(at), :] + coupled[block]
    start = [wide_ref[tile_at(2 * BLOCKS + block), :] for block in range(4 * BLOCKS)]
    first = [next_ref[tile_at(2 * BLOCKS + block), :] for block in range(4 * BLOCKS)]
    coupled = couple(inside, 4 * BLOCKS, next_ref, rows_ref, table_ref)
    second = []
    for block in range(4 * BLOCKS):
        image = screen_ref[tile_at(2 * BLOCKS + block), :] * first[block] + coupled[block]
        second.append(image)
        wide_ref[tile_at(block), :] = image
    for block in range(BLOCKS):
        first_ref[block] = next_ref[tile_at((2 + place) * BLOCKS + block), :]
        second_ref[block] = wide_ref[tile_at(place * BLOCKS + block), :]
    lane = lax.broadcasted_iota(jnp.int32, (1, 128), 1)
    line = jnp.zeros((1, 128), jnp.float32)
    pairs = ((start, start), (start, first), (first, first), (start, second), (first, second))
    for slot, (a, b) in enumerate(pairs):
        line = jnp.where(lane == slot, total(a, b, first_half), line)
    sums_ref[...] = jnp.broadcast_to(line, (32, 128))


def last_kernel(sums_ref, fields_ref, first_ref, second_ref, solution_ref, residual_ref, left_ref, right_ref):
    first_half = left_half()
    sums = jnp.sum(sums_ref[...], axis=0, keepdims=True)
    lane = lax.broadcasted_iota(jnp.int32, (1, 128), 1)

    def pick(place):
        return jnp.sum(jnp.where(lane == place, sums, 0.0), axis=1, keepdims=True)

    s00, s01, s11, s02, s12 = (pick(place) for place in range(5))
    alpha0 = s00 / s01
    norm1 = s00 - 2.0 * alpha0 * s01 + alpha0 * alpha0 * s11
    beta = norm1 / s00
    grow = 1.0 + beta
    curve = grow * grow * s01 - grow * alpha0 * (s02 + s11) + alpha0 * alpha0 * s12
    alpha1 = norm1 / curve
    for block in range(BLOCKS):
        start = doubled(fields_ref[block], first_half)
        first = first_ref[block]
        left = start - alpha0 * first
        direction = left + beta * start
        image = grow * first - alpha0 * second_ref[block]
        left_ref[block] = alpha0 * start + alpha1 * direction
        right_ref[block] = left - alpha1 * image
    for pair in range(4):
        lanes = slice(128 * pair, 128 * pair + 128)
        solution_ref[:, lanes] = jnp.where(first_half, left_ref[:, 2 * pair, :], left_ref[:, 2 * pair + 1, :])
        residual_ref[:, lanes] = jnp.where(first_half, right_ref[:, 2 * pair, :], right_ref[:, 2 * pair + 1, :])


def vmem(count):
    return [pl.BlockSpec(memory_space=pltpu.VMEM)] * count


def smem(count):
    return [pl.BlockSpec(memory_space=pltpu.SMEM)] * count


def shape(*dims):
    return pltpu.VMEM(dims, jnp.float32)


def resident(values):
    return pltpu.with_memory_space_constraint(values, pltpu.VMEM)


def per_device(positions, normals, weights, point_target, neighbours):
    table = resident(jnp.asarray(np.concatenate([plane_table()] * 2), jnp.bfloat16))
    parts = pl.pallas_call(
        splat_kernel,
        out_shape=shape(8 * SHARE, 128),
        in_specs=smem(1) + vmem(3),
        out_specs=vmem(1)[0],
        scratch_shapes=[pltpu.SMEM((8,), jnp.int32), pltpu.VMEM((8 * ROOM, 128), jnp.float32)],
        name="splat",
    )(point_target, positions.transpose(1, 0, 2), normals.transpose(1, 0, 2), weights)
    parts = lax.all_to_all(parts.reshape(8, 1, SHARE * 128), "scan", 0, 0, tiled=True)
    parts = resident(parts.reshape(8 * SHARE, 128))
    fields = resident(
        pl.pallas_call(
            combine_kernel,
            out_shape=shape(BLOCKS + 1, 8, 128),
            in_specs=vmem(2),
            out_specs=vmem(1)[0],
            name="combine",
        )(parts, resident(neighbours))
    )
    count = lax.axis_size("scan") * lax.axis_size("quad") * 4
    beside = resident(lax.ppermute(fields, ALL, [(i, (i - 4 if i % 4 < 2 else i + 4) % count) for i in range(count)]))
    packed, longer = pl.pallas_call(
        pack_kernel,
        out_shape=(shape(2 * BLOCKS + 1, 8, 128), shape(2 * BLOCKS + 2, 8, 128)),
        in_specs=vmem(2),
        out_specs=tuple(vmem(2)),
        name="pack",
    )(fields, beside)
    others = [
        resident(lax.ppermute(longer if step == 2 else packed, "place", [(i, i ^ step) for i in range(4)]))
        for step in (1, 2, 3)
    ]
    first, second, sums = pl.pallas_call(
        image_kernel,
        out_shape=(shape(BLOCKS, 8, 128), shape(BLOCKS, 8, 128), shape(32, 128)),
        in_specs=vmem(5),
        out_specs=tuple(vmem(3)),
        scratch_shapes=[
            pltpu.VMEM((8 * WINDOW + 8, 128), jnp.float32),
            pltpu.VMEM((8 * WINDOW + 8, 128), jnp.float32),
            pltpu.VMEM((8 * WINDOW, 128), jnp.float32),
            pltpu.VMEM((WINDOW, 128), jnp.int32),
            pltpu.VMEM((2 * BLOCKS, 128), jnp.int32),
            pltpu.SMEM((2 * BLOCKS, 128), jnp.int32),
            pltpu.VMEM((6 * BLOCKS * 16, 512), jnp.bfloat16),
            pltpu.SemaphoreType.DMA,
        ],
        name="images",
    )(resident(packed), *others, table)
    sums = resident(lax.all_to_all(sums, ("scan", "quad"), 0, 0, tiled=True))
    return pl.pallas_call(
        last_kernel,
        out_shape=(jax.ShapeDtypeStruct((BLOCKS, 512), jnp.float32),) * 2,
        in_specs=vmem(4),
        out_specs=tuple(vmem(2)),
        scratch_shapes=[pltpu.VMEM((BLOCKS, 8, 128), jnp.float32)] * 2,
        name="last",
    )(sums, fields, resident(first), resident(second))


def solution(mesh):
    scan, morton = mesh.devices.shape
    grouped = Mesh(mesh.devices.reshape(scan, morton // 4, 4), ALL)
    placed = (P(ALL, None, None), P(ALL, None, None), P(ALL, None), P(ALL), P(ALL, None))
    return jax.shard_map(
        per_device,
        mesh=grouped,
        in_specs=placed,
        out_specs=(P(ALL, None), P(ALL, None)),
        check_vma=False,
    )
```
